32 devices in a mesh: brick: 8 (over z, y), mp: 4 (over x, core).
Axes of the slice: x: 2, y: 2, z: 4, core: 2. Of those that a mesh axis runs over, the one named last changes fastest.
Arguments:
- voxel_feats: bfloat16 [24576, 512], P('brick'), may hold values from -6 to 6
- slot_rank: int32 [24576], P('brick'), may hold values from 0 to 16384, as said below
- curve_order: int32 [16384], P('brick'), may hold values from 0 to 24575, as said below
- patch_shift: int32 [1], replicated, may hold values from 1 to 1023
- qkv_weight: bfloat16 [512, 1536], P(None, 'mp')
- proj_weight: bfloat16 [512, 512], P('mp'), may hold values from -0.25 to 0.25
- up_weight: bfloat16 [512, 2048], P(None, 'mp'), may hold values from -0.25 to 0.25
- down_weight: bfloat16 [2048, 512], P('mp'), may hold values from -0.125 to 0.125
- norm_gains: float32 [2, 512], replicated, may hold values from 0.25 to 1.75
Outputs:
- voxel_out: bfloat16 [24576, 512], P('brick', 'mp')
The draws below stay inside these ranges and needn't reach their ends.
Inputs may be any that keep to these rules, and one draw needn't show every extreme that they name: `slot_rank`: within each brick's 3072 slots the occupied ones come first and hold distinct curve positions in increasing order; the rest hold 16384. Every curve position lies in exactly one slot. Curve shard k is positions k * 2048 to (k + 1) * 2048 - 1 and draws its voxels only from bricks k - 1, k, k + 1 and k + 2 (mod 8). A brick holds at most 768 voxels of one shard, and some brick holds exactly 768 of some shard; some brick has all 3072 slots occupied. curve_order[p] = brick * 3072 + slot of the voxel at curve position p, the inverse of slot_rank on occupied slots.
All inputs are finite; a program needn't handle non-finite values.
Results may differ from the reference program's by a relative error of at most 0.012.
The reference program's roundings to bfloat16 on the way count: a program that leaves them out, or rounds other values in their place, can miss the bound.
Values may be sent and summed in bfloat16 or wider, within the bound.
A program may use at most 128 MiB of HBM per device.

```python
import math
import jax
import jax.numpy as jnp
import numpy as np
from jax import lax

C = 512
HEADS = 32
HID = 2048
PATCH = 1024
TOK_DEV = 2048
BRICKS = 8
TOKENS = 16384
CAP = 3072
N_MP = 4


def pattern_table():
    grid = np.stack(np.meshgrid(np.arange(1, 4), np.arange(1, 4), np.arange(1, 4), np.arange(1, 4), indexing='ij'), -1).reshape(-1, 4)
    return grid[grid.sum(axis=1) == 8].astype(np.int32)


def layout_tables(key):
    root = jax.random.fold_in(key, 911)
    table = jnp.asarray(pattern_table())
    picks = jax.random.randint(jax.random.fold_in(root, 1), (BRICKS,), 0, table.shape[0])
    shares = table[picks]
    shares = shares.at[1].set(jnp.array([3, 1, 1, 3], jnp.int32))
    shares = shares.at[0].set(jnp.array([1, 3, 3, 1], jnp.int32))
    shares = shares.at[BRICKS - 1].set(jnp.array([1, 1, 3, 3], jnp.int32))
    shares = shares.at[BRICKS - 2].set(jnp.array([2, 1, 2, 3], jnp.int32))
    unit_rows = TOK_DEV // 8
    ends = jnp.cumsum(shares * unit_rows, axis=1).astype(jnp.int32)
    spots = jnp.arange(TOK_DEV, dtype=jnp.int32)
    lanes = jnp.sum((ends[:, None, :] <= spots[None, :, None]).astype(jnp.int32), axis=2).astype(jnp.int32)
    shard_ids = jnp.arange(BRICKS, dtype=jnp.int32)
    labels = ((shard_ids[:, None] + lanes - 1) % BRICKS).reshape(-1).astype(jnp.int32)
    order = jnp.argsort(labels, stable=True).astype(jnp.int32)
    brick_count = jnp.bincount(labels, length=BRICKS).astype(jnp.int32)
    brick_start = (jnp.cumsum(brick_count) - brick_count).astype(jnp.int32)
    sorted_labels = labels[order]
    slot_index = jnp.arange(TOKENS, dtype=jnp.int32) - brick_start[sorted_labels]
    global_slot = (sorted_labels * CAP + slot_index).astype(jnp.int32)
    curve_order = jnp.zeros((TOKENS,), jnp.int32).at[order].set(global_slot)
    slot_rank = jnp.full((BRICKS * CAP,), TOKENS, jnp.int32).at[global_slot].set(order)
    return (slot_rank, curve_order)


def draw_slot_rank(key, part):
    return layout_tables(key)[0]


def draw_curve_order(key, part):
    return layout_tables(key)[1]


def draw_qkv_weight(key, part):
    weights_full = jax.random.normal(jax.random.fold_in(key, 17), (C, 3 * C), jnp.float32) * C ** (-0.5)
    return weights_full.astype(jnp.bfloat16)


def level_of(own_key, dims, cuts, smallest, high):
    factor_of, own = 1.0, jax.random.fold_in(own_key, 6)
    for position, shards_of in cuts:
        heights = jnp.exp(jax.random.uniform(jax.random.fold_in(own, position), (shards_of,), jnp.float32, smallest / len(cuts), high / len(cuts)))
        factor_of = factor_of * jnp.repeat(heights, dims[position] // shards_of).reshape([-1 if axis == position else 1 for axis in range(len(dims))])
    return factor_of


def normal_values(own_key, shape, scale, most, cuts=(), held_as=jnp.bfloat16):
    values = jax.random.normal(own_key, shape, jnp.float32) * scale
    if len(cuts) > 0:
        values = level_of(own_key, shape, cuts, -0.22, 0.18) * values
    return jnp.clip(values, min=-most, max=most).astype(held_as)


def setup_inputs(seed: int = 0) -> dict:
    key_list = jax.random.split(jax.random.key(seed), 10)
    voxel_feats = normal_values(key_list[0], (BRICKS * CAP, C), 1.0, 6.0, ((0, 8),))
    slot_rank = draw_slot_rank(jax.random.fold_in(key_list[9], 71), 0)
    curve_order = draw_curve_order(jax.random.fold_in(key_list[9], 71), 0)
    patch_shift = jax.random.randint(key_list[3], (1,), 1, PATCH).astype(jnp.int32)
    qkv_weight = draw_qkv_weight(jax.random.fold_in(key_list[9], 71), 0)
    proj_weight = normal_values(key_list[5], (C, C), C ** -0.5, 0.25, ((0, 4),))
    up_weight = normal_values(key_list[6], (C, HID), C ** -0.5, 0.25, ((1, 4),))
    down_weight = normal_values(key_list[7], (HID, C), HID ** -0.5, 0.125, ((0, 4),))
    norm_gains = jnp.clip(1.0 + 0.15 * jax.random.normal(key_list[8], (2, C), jnp.float32), 0.25, 1.75)
    return dict(voxel_feats=voxel_feats, slot_rank=slot_rank, curve_order=curve_order, patch_shift=patch_shift, qkv_weight=qkv_weight, proj_weight=proj_weight, up_weight=up_weight, down_weight=down_weight, norm_gains=norm_gains)


EPSILON = 1e-05

def layer_norm(values, gain):
    values = values.astype(jnp.float32)
    centred = values - lax.optimization_barrier(jnp.mean(values, axis=-1, keepdims=True))
    spread = lax.optimization_barrier(jnp.mean(centred * centred, axis=-1, keepdims=True))
    return (centred * lax.rsqrt(spread + EPSILON) * gain).astype(jnp.bfloat16)

def patch_attention(qkv_rows, heads_here, patch_len):
    row_count = qkv_rows.shape[0]
    head_dim = qkv_rows.shape[1] // (3 * heads_here)
    group_size = math.gcd(heads_here, 4)
    group_count = heads_here // group_size
    scale = head_dim ** (-0.5)

    def one_group(piece):
        query = piece[:, :, 0].astype(jnp.float32)
        keys_here = piece[:, :, 1].astype(jnp.float32)
        values_here = piece[:, :, 2].astype(jnp.float32)
        scores = jnp.einsum('qhd,khd->hqk', query, keys_here) * scale
        highest = lax.optimization_barrier(jnp.max(scores, axis=-1, keepdims=True))
        weights_exp = jnp.exp(scores - highest)
        softmax_weights = (weights_exp / lax.optimization_barrier(jnp.sum(weights_exp, axis=-1, keepdims=True))).astype(jnp.bfloat16)
        return jnp.einsum('hqk,khd->qhd', softmax_weights.astype(jnp.float32), values_here).astype(jnp.bfloat16)

    def one_patch(block):
        pieces = jnp.moveaxis(block.reshape(patch_len, group_count, group_size, 3, head_dim), 1, 0)
        outputs = lax.map(one_group, pieces)
        return jnp.moveaxis(outputs, 0, 1).reshape(patch_len, heads_here * head_dim)
    blocks = qkv_rows.reshape(row_count // patch_len, patch_len, qkv_rows.shape[1])
    return lax.map(one_patch, blocks).reshape(row_count, heads_here * head_dim)

def partial_sum_rounded(left, right, groups):
    width = left.shape[1] // groups
    total = jnp.zeros((left.shape[0], right.shape[1]), jnp.float32)
    for group_index in range(groups):
        term = jnp.dot(left[:, group_index * width:(group_index + 1) * width], right[group_index * width:(group_index + 1) * width], preferred_element_type=jnp.float32).astype(jnp.bfloat16)
        total = total + lax.optimization_barrier(term).astype(jnp.float32)
    return total

def reference(voxel_feats, slot_rank, curve_order, patch_shift, qkv_weight, proj_weight, up_weight, down_weight, norm_gains):
    curve = voxel_feats[curve_order]
    normed = layer_norm(curve, norm_gains[0])
    qkv_rows = jnp.dot(normed, qkv_weight, preferred_element_type=jnp.float32).astype(jnp.bfloat16)
    offset = patch_shift[0]
    rolled = jnp.roll(qkv_rows, -offset, axis=0)
    attended = jnp.roll(patch_attention(rolled, HEADS, PATCH), offset, axis=0)
    mixed = partial_sum_rounded(attended, proj_weight, N_MP)
    hidden_state = (curve.astype(jnp.float32) + mixed).astype(jnp.bfloat16)
    normed_two = layer_norm(hidden_state, norm_gains[1])
    expanded = jax.nn.gelu(jnp.dot(normed_two, up_weight, preferred_element_type=jnp.float32), approximate=False).astype(jnp.bfloat16)
    mlp_sum = partial_sum_rounded(expanded, down_weight, N_MP)
    result = (hidden_state.astype(jnp.float32) + mlp_sum).astype(jnp.bfloat16)
    live_slots = slot_rank < TOKENS
    picked = result[jnp.minimum(slot_rank, TOKENS - 1)]
    return jnp.where(live_slots[:, None], picked, jnp.zeros_like(picked))
```

```python
import functools
import math

import jax
import jax.numpy as jnp
from jax import lax
from jax.experimental import pallas as pl
from jax.experimental.pallas import tpu as pltpu
from jax.sharding import PartitionSpec as P

HEADS = 32
PATCH = 1024
EPSILON = 1e-05
VMEM_BYTES = 56 * 1024 * 1024


def shifted(value, axis, steps):
    count = lax.axis_size(axis)
    pairs = [(source, (source + steps) % count) for source in range(count)]
    return lax.ppermute(value, axis, pairs)


def layer_norm(values, gain):
    centred = values - jnp.mean(values, axis=-1, keepdims=True)
    spread = jnp.mean(centred * centred, axis=-1, keepdims=True)
    return (centred * lax.rsqrt(spread + EPSILON) * gain).astype(jnp.bfloat16)


def attention_kernel(
    head_dim,
    query_tile,
    query_from,
    patch_rows,
    gain,
    weights,
    attended,
    normed,
    queries,
    keys,
    values,
):
    groups, _, triple = weights.shape
    lanes = triple // 3
    group_heads = lanes // head_dim
    query_rows = attended.shape[0]
    normed[...] = layer_norm(patch_rows[...].astype(jnp.float32), gain[...])
    start = pl.multiple_of(query_from[0], query_rows)
    scale = head_dim ** (-0.5) * math.log2(math.e)
    lane_head = lax.broadcasted_iota(jnp.int32, (1, lanes), 1) // head_dim
    for group in range(groups):
        weight = weights[group]
        queries[group] = (
            jnp.dot(
                normed[pl.ds(start, query_rows), :],
                weight[:, :lanes],
                preferred_element_type=jnp.float32,
            )
            * scale
        ).astype(jnp.bfloat16)
        both = jnp.dot(
            normed[...], weight[:, lanes:], preferred_element_type=jnp.float32
        ).astype(jnp.bfloat16)
        keys[group] = both[:, :lanes]
        values[group, :, :lanes] = both[:, lanes:]
        values[group, :, lanes:] = jnp.ones_like(both[:, lanes:])

    def one_group(group, carry):
        attended_group = [
            jnp.zeros((query_tile, lanes), jnp.float32)
            for _ in range(query_rows // query_tile)
        ]

        def one_head(head, sums):
            mine = lane_head == head
            results = []
            for tile in range(query_rows // query_tile):
                query = queries[group, tile * query_tile : (tile + 1) * query_tile, :]
                query = jnp.where(mine, query, jnp.zeros_like(query))
                scores = lax.dot_general(
                    query,
                    keys[group],
                    (((1,), (1,)), ((), ())),
                    preferred_element_type=jnp.float32,
                )
                highest = jnp.max(scores, axis=-1, keepdims=True)
                exps = jnp.exp2(scores - highest).astype(jnp.bfloat16)
                product = jnp.dot(
                    exps, values[group], preferred_element_type=jnp.float32
                )
                result = product[:, :lanes] / product[:, lanes:]
                results.append(jnp.where(mine, result, sums[tile]))
            return tuple(results)

        sums = lax.fori_loop(0, group_heads, one_head, tuple(attended_group))
        for tile in range(query_rows // query_tile):
            attended[tile * query_tile : (tile + 1) * query_tile, pl.ds(
                pl.multiple_of(group * lanes, lanes), lanes
            )] = sums[tile].astype(jnp.bfloat16)
        return carry

    lax.fori_loop(0, groups, one_group, 0)


def attention(patch_rows, gain, weights, query_from, query_rows, head_dim):
    groups, width, triple = weights.shape
    lanes = triple // 3
    rows = patch_rows.shape[0]
    whole = pl.BlockSpec(memory_space=pltpu.VMEM)
    return pl.pallas_call(
        functools.partial(attention_kernel, head_dim, query_rows // 4),
        out_shape=jax.ShapeDtypeStruct((query_rows, groups * lanes), jnp.bfloat16),
        in_specs=[pl.BlockSpec(memory_space=pltpu.SMEM), whole, whole, whole],
        out_specs=whole,
        scratch_shapes=[
            pltpu.VMEM((rows, width), jnp.bfloat16),
            pltpu.VMEM((groups, query_rows, lanes), jnp.bfloat16),
            pltpu.VMEM((groups, rows, lanes), jnp.bfloat16),
            pltpu.VMEM((groups, rows, 2 * lanes), jnp.bfloat16),
        ],
        compiler_params=pltpu.CompilerParams(vmem_limit_bytes=VMEM_BYTES),
        cost_estimate=pl.CostEstimate(
            flops=4 * rows * query_rows * groups * lanes * 16,
            bytes_accessed=4 * rows * width,
            transcendentals=rows * query_rows * groups * 8,
        ),
    )(query_from, patch_rows, gain, weights)


def mlp_kernel(
    query_from, patch_rows, attended, gain, proj_weight, up_weight, down_weight, result
):
    groups, depth, _ = proj_weight.shape
    rows = attended.shape[0]
    start = pl.multiple_of(query_from[0], rows)
    own = patch_rows[pl.ds(start, rows), :].astype(jnp.float32)
    mixed = None
    for group in range(groups):
        term = jnp.dot(
            attended[:, group * depth : (group + 1) * depth],
            proj_weight[group],
            preferred_element_type=jnp.float32,
        ).astype(jnp.bfloat16).astype(jnp.float32)
        mixed = term if mixed is None else mixed + term
    hidden = (own + mixed).astype(jnp.bfloat16).astype(jnp.float32)
    normed = layer_norm(hidden, gain[...])
    total = None
    for group in range(groups):
        expanded = jnp.dot(normed, up_weight[group], preferred_element_type=jnp.float32)
        expanded = (
            0.5 * expanded * (1.0 + lax.erf(expanded * math.sqrt(0.5)))
        ).astype(jnp.bfloat16)
        term = jnp.dot(
            expanded, down_weight[group], preferred_element_type=jnp.float32
        ).astype(jnp.bfloat16).astype(jnp.float32)
        total = term if total is None else total + term
    result[...] = (hidden + total).astype(jnp.bfloat16)


def mlp(patch_rows, attended, gain, proj_weight, up_weight, down_weight, query_from):
    whole = pl.BlockSpec(memory_space=pltpu.VMEM)
    rows, width = attended.shape
    groups, _, hidden = up_weight.shape
    return pl.pallas_call(
        mlp_kernel,
        out_shape=jax.ShapeDtypeStruct(attended.shape, jnp.bfloat16),
        in_specs=[pl.BlockSpec(memory_space=pltpu.SMEM)] + [whole] * 6,
        out_specs=whole,
        compiler_params=pltpu.CompilerParams(vmem_limit_bytes=VMEM_BYTES),
        cost_estimate=pl.CostEstimate(
            flops=4 * rows * width * hidden * groups,
            bytes_accessed=8 * width * hidden * groups,
            transcendentals=rows * hidden * groups,
        ),
    )(query_from, patch_rows, attended, gain, proj_weight, up_weight, down_weight)


def per_device(
    voxel_feats,
    slot_rank,
    curve_order,
    patch_shift,
    qkv_weight,
    proj_weight,
    up_weight,
    down_weight,
    norm_gains,
):
    bricks = lax.axis_size("brick")
    model_parts = lax.axis_size("mp")
    my_index = lax.axis_index("brick")
    part_index = lax.axis_index("mp")
    capacity = voxel_feats.shape[0]
    shard_rows = curve_order.shape[0]
    pair_rows = 3 * (shard_rows // 8)
    width_full = voxel_feats.shape[1]
    width_part = width_full // model_parts
    quarter_rows = shard_rows // model_parts
    head_dim = width_full // HEADS
    offset = patch_shift[0]
    latest = capacity - pair_rows

    triple = qkv_weight.shape[1]
    spot = jnp.arange(triple, dtype=jnp.int32)
    kind, within = spot // width_part, spot % width_part
    origin = (within // head_dim) * 3 * head_dim + kind * head_dim + within % head_dim
    shuffle = (spot[:, None] == origin[None, :]).astype(jnp.bfloat16)
    qkv_sorted = jnp.dot(
        qkv_weight, shuffle, preferred_element_type=jnp.float32
    ).astype(jnp.bfloat16)
    qkv_all = lax.all_gather(qkv_sorted, "mp", axis=0)
    proj_all = lax.all_gather(proj_weight, "mp", axis=0)
    up_all = lax.all_gather(up_weight, "mp", axis=0)
    down_all = lax.all_gather(down_weight, "mp", axis=0)

    lane_ids = jnp.arange(4, dtype=jnp.int32)
    lane_targets = (my_index - (lane_ids - 1)) % bricks
    run_starts = jnp.sum(
        (slot_rank[:, None] < (lane_targets * shard_rows)[None, :]).astype(jnp.int32), axis=0
    )
    slab_starts = jnp.minimum(run_starts, latest)
    source_brick = curve_order // capacity
    source_slot = curve_order % capacity
    source_lane = (source_brick - my_index + 1) % bricks
    from_lane = source_lane[:, None] == lane_ids[None, :]
    first_slot = jnp.min(jnp.where(from_lane, source_slot[:, None], capacity), axis=0)
    first_slot = jnp.minimum(first_slot, latest)
    first_of_row = jnp.sum(jnp.where(from_lane, first_slot[None, :], 0), axis=1)
    recv_index = source_lane * pair_rows + source_slot - first_of_row
    select = (
        recv_index[:, None] == jnp.arange(4 * pair_rows, dtype=jnp.int32)[None, :]
    ).astype(jnp.bfloat16)

    lanes_in = []
    for lane in range(4):
        piece = lax.dynamic_slice(
            voxel_feats,
            (slab_starts[lane], part_index * width_part),
            (pair_rows, width_part),
        )
        if lane != 1:
            piece = shifted(piece, "brick", 1 - lane)
        lanes_in.append(piece)
    local_part = jnp.dot(
        select, jnp.concatenate(lanes_in, axis=0), preferred_element_type=jnp.float32
    ).astype(jnp.bfloat16)
    head_next = shifted(local_part[:PATCH], "brick", -1)
    window = lax.dynamic_slice_in_dim(
        jnp.concatenate([local_part, head_next], axis=0), offset, shard_rows, 0
    )

    def patch_of(part):
        return (part * quarter_rows) // PATCH

    pieces = []
    for step in range(model_parts):
        target = (part_index + step) % model_parts
        piece = lax.dynamic_slice_in_dim(window, patch_of(target) * PATCH, PATCH, 0)
        if step:
            piece = shifted(piece, "mp", step)
        pieces.append(piece)
    patch_rows = jnp.zeros((PATCH, width_full), jnp.bfloat16)
    for step in range(model_parts):
        source = (part_index - step) % model_parts
        patch_rows = lax.dynamic_update_slice_in_dim(
            patch_rows, pieces[step], source * width_part, 1
        )
    query_from = ((part_index * quarter_rows) % PATCH)[None]
    attended = attention(
        patch_rows, norm_gains[0:1], qkv_all, query_from, quarter_rows, head_dim
    )
    result = mlp(
        patch_rows, attended, norm_gains[1:2], proj_all, up_all, down_all, query_from
    )

    result_window = jnp.zeros((shard_rows, width_part), jnp.bfloat16)
    for step in range(model_parts):
        target = (part_index + step) % model_parts
        piece = lax.dynamic_slice_in_dim(result, target * width_part, width_part, 1)
        if step:
            piece = shifted(piece, "mp", step)
        source = (part_index - step) % model_parts
        result_window = lax.dynamic_update_slice_in_dim(
            result_window, piece, source * quarter_rows, 0
        )
    tail_rows = shifted(result_window[shard_rows - PATCH :], "brick", 1)
    own_rows = lax.dynamic_slice_in_dim(
        jnp.concatenate([tail_rows, result_window], axis=0), PATCH - offset, shard_rows, 0
    )
    back_rows = lax.dot_general(
        select, own_rows, (((0,), (0,)), ((), ())), preferred_element_type=jnp.float32
    ).astype(jnp.bfloat16)
    out = jnp.zeros((capacity, width_part), jnp.bfloat16)
    for lane in range(4):
        piece = back_rows[lane * pair_rows : (lane + 1) * pair_rows]
        if lane != 1:
            piece = shifted(piece, "brick", lane - 1)
        before = lax.dynamic_slice_in_dim(out, slab_starts[lane], pair_rows, 0)
        out = lax.dynamic_update_slice_in_dim(out, before + piece, slab_starts[lane], 0)
    return out


def solution(mesh):
    return jax.shard_map(
        per_device,
        mesh=mesh,
        in_specs=(
            P("brick", None),
            P("brick"),
            P("brick"),
            P(),
            P(None, "mp"),
            P("mp", None),
            P(None, "mp"),
            P("mp", None),
            P(),
        ),
        out_specs=P("brick", "mp"),
        check_vma=False,
    )
```

```python
import functools
import math

import jax
import jax.numpy as jnp
from jax import lax
from jax.experimental import pallas as pl
from jax.experimental.pallas import tpu as pltpu
from jax.sharding import PartitionSpec as P

HEADS = 32
PATCH = 1024
EPSILON = 1e-05
VMEM_BYTES = 56 * 1024 * 1024


MESH = pl.DeviceIdType.MESH


def wrapped(value, count):
    value = jnp.where(value < 0, value + count, value)
    return jnp.where(value >= count, value - count, value)


def greet_all(bricks, parts):
    brick, part = lax.axis_index("brick"), lax.axis_index("mp")
    barrier = pltpu.get_barrier_semaphore()
    peers = [(0, step) for step in range(1, parts)]
    peers += [(away, step) for away in (-1, 1) for step in range(parts)]
    peers += [(-2, 0), (2, 0)]
    for away, step in peers:
        pl.semaphore_signal(
            barrier,
            inc=1,
            device_id=(lax.rem(brick + away + bricks, bricks), lax.rem(part + step, parts)),
            device_id_type=MESH,
        )
    pl.semaphore_wait(barrier, len(peers))


def enter_kernel(
    bricks,
    parts,
    index,
    slabs,
    patch_rows,
    arrived,
    total,
    merged,
    window_in,
    head_in,
    lane_send,
    lane_recv,
    window_send,
    window_recv,
    head_send,
    head_recv,
):
    brick, part = lax.axis_index("brick"), lax.axis_index("mp")
    slab_rows, width = slabs.shape[1], slabs.shape[2]
    rows = index.shape[0]
    tile = 512
    quarter = (rows - PATCH) // parts
    greet_all(bricks, parts)

    def lane_copy(lane):
        return pltpu.make_async_remote_copy(
            src_ref=slabs.at[lane],
            dst_ref=arrived.at[lane],
            send_sem=lane_send.at[lane],
            recv_sem=lane_recv.at[lane],
            device_id=(lax.rem(brick - lane + 1 + bricks, bricks), part),
            device_id_type=MESH,
        )

    for lane in (3, 0, 2):
        lane_copy(lane).start()

    def merge(lane, source, first):
        def one_tile(step, carry):
            at = pl.ds(pl.multiple_of(step * tile, tile), tile)
            spots = lax.broadcasted_iota(jnp.int32, (tile, slab_rows), 1) + lane * slab_rows
            chosen = (index[at, :] == spots).astype(jnp.bfloat16)
            term = jnp.dot(chosen, source, preferred_element_type=jnp.float32)
            if first:
                total[at, :] = term
            else:
                total[at, :] += term
            return carry

        lax.fori_loop(0, rows // tile, one_tile, 0)

    merge(1, slabs[1], True)
    for lane in (2, 0, 3):
        lane_copy(lane).wait()
        merge(lane, arrived[lane], False)
    merged[...] = total[...].astype(jnp.bfloat16)

    def patch_start(target):
        return pl.multiple_of((target * quarter // PATCH + 1) * PATCH, PATCH)

    last = rows - PATCH

    def head_copy(step):
        target = lax.rem(part + step, parts)
        return pltpu.make_async_remote_copy(
            src_ref=merged.at[pl.ds(0, PATCH)],
            dst_ref=head_in.at[step],
            send_sem=head_send.at[step],
            recv_sem=head_recv.at[step],
            device_id=(lax.rem(brick - 1 + bricks, bricks), target),
            device_id_type=MESH,
        )

    def window_copy(step):
        target = lax.rem(part + step, parts)
        return pltpu.make_async_remote_copy(
            src_ref=merged.at[pl.ds(patch_start(target), PATCH)],
            dst_ref=window_in.at[step],
            send_sem=window_send.at[step],
            recv_sem=window_recv.at[step],
            device_id=(brick, target),
            device_id_type=MESH,
        )

    for step in range(parts):

        @pl.when(patch_start(lax.rem(part + step, parts)) == last)
        def _():
            head_copy(step).start()

    for step in range(1, parts):
        window_copy(step).start()

    def columns(step):
        source = lax.rem(part - step + parts, parts)
        return pl.ds(pl.multiple_of(source * width, width), width)

    patch_rows[:, columns(0)] = merged[pl.ds(patch_start(part), PATCH), :]
    for step in range(1, parts):
        window_copy(step).wait()
        patch_rows[:, columns(step)] = window_in[step]

    @pl.when(patch_start(part) == last)
    def _():
        for step in range(parts):
            head_copy(step).wait_recv()
            patch_rows[:, columns(step)] += head_in[step]

    for step in range(parts):

        @pl.when(patch_start(lax.rem(part + step, parts)) == last)
        def _():
            head_copy(step).wait_send()


def enter(index, slabs, bricks, parts):
    lanes, slab_rows, width = slabs.shape
    rows = index.shape[0]
    whole = pl.BlockSpec(memory_space=pltpu.VMEM)
    return pl.pallas_call(
        functools.partial(enter_kernel, bricks, parts),
        out_shape=jax.ShapeDtypeStruct((PATCH, width * parts), jnp.bfloat16),
        in_specs=[whole, whole],
        out_specs=whole,
        scratch_shapes=[
            pltpu.VMEM((lanes, slab_rows, width), jnp.bfloat16),
            pltpu.VMEM((rows, width), jnp.float32),
            pltpu.VMEM((rows, width), jnp.bfloat16),
            pltpu.VMEM((parts, PATCH, width), jnp.bfloat16),
            pltpu.VMEM((parts, PATCH, width), jnp.bfloat16),
            pltpu.SemaphoreType.DMA((lanes,)),
            pltpu.SemaphoreType.DMA((lanes,)),
            pltpu.SemaphoreType.DMA((parts,)),
            pltpu.SemaphoreType.DMA((parts,)),
            pltpu.SemaphoreType.DMA((parts,)),
            pltpu.SemaphoreType.DMA((parts,)),
        ],
        compiler_params=pltpu.CompilerParams(
            collective_id=0, has_side_effects=True, vmem_limit_bytes=VMEM_BYTES
        ),
        cost_estimate=pl.CostEstimate(
            flops=2 * rows * lanes * slab_rows * width,
            bytes_accessed=20 * slab_rows * width * lanes,
            transcendentals=0,
        ),
    )(index, slabs)


def leave_kernel(
    bricks,
    parts,
    index,
    place,
    result,
    out,
    rows_in,
    leaving,
    arrived,
    total,
    window_send,
    window_recv,
    tail_send,
    tail_recv,
    lane_send,
    lane_recv,
):
    brick, part = lax.axis_index("brick"), lax.axis_index("mp")
    lanes, slab_rows, width = leaving.shape
    quarter = result.shape[1]
    capacity = out.shape[0]
    rows = rows_in.shape[0]
    tile = 512
    last = rows - PATCH
    greet_all(bricks, parts)

    def row_start(source):
        return PATCH + source * quarter

    def tail_copy(step):
        target = lax.rem(part + step, parts)
        start = pl.multiple_of(jnp.maximum(row_start(part) - last, 0), quarter)
        return pltpu.make_async_remote_copy(
            src_ref=result.at[target],
            dst_ref=rows_in.at[pl.ds(start, quarter)],
            send_sem=tail_send.at[step],
            recv_sem=tail_recv.at[part],
            device_id=(lax.rem(brick + 1, bricks), target),
            device_id_type=MESH,
        )

    def window_copy(step):
        target = lax.rem(part + step, parts)
        start = pl.multiple_of(row_start(part), quarter)
        return pltpu.make_async_remote_copy(
            src_ref=result.at[target],
            dst_ref=rows_in.at[pl.ds(start, quarter)],
            send_sem=window_send.at[step],
            recv_sem=window_recv.at[step],
            device_id=(brick, target),
            device_id_type=MESH,
        )

    def tail_arrival(source):
        return pltpu.make_async_remote_copy(
            src_ref=result.at[0],
            dst_ref=rows_in.at[pl.ds(row_start(source) - last, quarter)],
            send_sem=tail_send.at[0],
            recv_sem=tail_recv.at[source],
            device_id=(lax.rem(brick + 1, bricks), part),
            device_id_type=MESH,
        )

    def window_arrival(step):
        source = lax.rem(part - step + parts, parts)
        return pltpu.make_async_remote_copy(
            src_ref=result.at[0],
            dst_ref=rows_in.at[pl.ds(pl.multiple_of(row_start(source), quarter), quarter)],
            send_sem=window_send.at[step],
            recv_sem=window_recv.at[step],
            device_id=(brick, source),
            device_id_type=MESH,
        )

    sends_tail = row_start(part) >= last

    @pl.when(sends_tail)
    def _():
        for step in range(parts):
            tail_copy(step).start()

    for step in range(1, parts):
        window_copy(step).start()
    rows_in[pl.ds(pl.multiple_of(row_start(part), quarter), quarter), :] = result[part]
    for step in range(1, parts):
        window_arrival(step).wait_recv()
    for source in range(parts):
        if row_start(source) >= last:
            tail_arrival(source).wait_recv()

    def lane_copy(lane):
        return pltpu.make_async_remote_copy(
            src_ref=leaving.at[lane],
            dst_ref=arrived.at[lane],
            send_sem=lane_send.at[lane],
            recv_sem=lane_recv.at[lane],
            device_id=(lax.rem(brick + lane - 1 + bricks, bricks), part),
            device_id_type=MESH,
        )

    third = slab_rows // 3

    def spread(lane):
        def one_tile(step, carry):
            start = pl.multiple_of(step * third, third)
            spots = (
                lax.broadcasted_iota(jnp.int32, (third, rows), 0) + lane * slab_rows + start
            )
            chosen = (index[...] == spots).astype(jnp.bfloat16)
            leaving[lane, pl.ds(start, third), :] = jnp.dot(
                chosen, rows_in[...], preferred_element_type=jnp.float32
            ).astype(jnp.bfloat16)
            return carry

        lax.fori_loop(0, 3, one_tile, 0)

    for lane in (3, 0, 2):
        spread(lane)
        lane_copy(lane).start()
    spread(1)

    def put(lane, source, first, final):
        def one_tile(step, carry):
            at = pl.ds(pl.multiple_of(step * tile, tile), tile)
            spots = lax.broadcasted_iota(jnp.int32, (tile, slab_rows), 1) + lane * slab_rows
            chosen = (place[at, :] == spots).astype(jnp.bfloat16)
            term = jnp.dot(chosen, source, preferred_element_type=jnp.float32)
            if not first:
                term = total[at, :] + term
            if final:
                out[at, :] = term.astype(jnp.bfloat16)
            else:
                total[at, :] = term
            return carry

        lax.fori_loop(0, capacity // tile, one_tile, 0)

    put(1, leaving[1], True, False)
    for lane in (2, 0, 3):
        lane_copy(lane).wait()
        put(lane, arrived[lane], False, lane == 3)

    for step in range(1, parts):
        window_copy(step).wait_send()

    @pl.when(sends_tail)
    def _():
        for step in range(parts):
            tail_copy(step).wait_send()


def leave(index, place, result, bricks, lanes, slab_rows):
    parts, quarter, width = result.shape
    rows = index.shape[1]
    capacity = place.shape[0]
    whole = pl.BlockSpec(memory_space=pltpu.VMEM)
    return pl.pallas_call(
        functools.partial(leave_kernel, bricks, parts),
        out_shape=jax.ShapeDtypeStruct((capacity, width), jnp.bfloat16),
        in_specs=[whole, whole, whole],
        out_specs=whole,
        scratch_shapes=[
            pltpu.VMEM((rows, width), jnp.bfloat16),
            pltpu.VMEM((lanes, slab_rows, width), jnp.bfloat16),
            pltpu.VMEM((lanes, slab_rows, width), jnp.bfloat16),
            pltpu.VMEM((capacity, width), jnp.float32),
            pltpu.SemaphoreType.DMA((parts,)),
            pltpu.SemaphoreType.DMA((parts,)),
            pltpu.SemaphoreType.DMA((parts,)),
            pltpu.SemaphoreType.DMA((parts,)),
            pltpu.SemaphoreType.DMA((lanes,)),
            pltpu.SemaphoreType.DMA((lanes,)),
        ],
        compiler_params=pltpu.CompilerParams(
            collective_id=1, has_side_effects=True, vmem_limit_bytes=VMEM_BYTES
        ),
        cost_estimate=pl.CostEstimate(
            flops=4 * rows * lanes * slab_rows * width,
            bytes_accessed=20 * slab_rows * width * lanes,
            transcendentals=0,
        ),
    )(index, place, result)


def layer_norm(values, gain):
    centred = values - jnp.mean(values, axis=-1, keepdims=True)
    spread = jnp.mean(centred * centred, axis=-1, keepdims=True)
    return (centred * lax.rsqrt(spread + EPSILON) * gain).astype(jnp.bfloat16)


def attention_kernel(
    head_dim,
    query_tile,
    query_from,
    patch_rows,
    gain,
    weights,
    attended,
    normed,
    queries,
    keys,
    values,
):
    groups, _, triple = weights.shape
    lanes = triple // 3
    group_heads = lanes // head_dim
    query_rows = attended.shape[0]
    normed[...] = layer_norm(patch_rows[...].astype(jnp.float32), gain[...])
    start = pl.multiple_of(query_from[0], query_rows)
    scale = head_dim ** (-0.5) * math.log2(math.e)
    lane_head = lax.broadcasted_iota(jnp.int32, (1, lanes), 1) // head_dim
    for group in range(groups):
        weight = weights[group]
        queries[group] = (
            jnp.dot(
                normed[pl.ds(start, query_rows), :],
                weight[:, :lanes],
                preferred_element_type=jnp.float32,
            )
            * scale
        ).astype(jnp.bfloat16)
        both = jnp.dot(
            normed[...], weight[:, lanes:], preferred_element_type=jnp.float32
        ).astype(jnp.bfloat16)
        keys[group] = both[:, :lanes]
        values[group, :, :lanes] = both[:, lanes:]
        values[group, :, lanes:] = jnp.ones_like(both[:, lanes:])

    def one_group(group, carry):
        attended_group = [
            jnp.zeros((query_tile, lanes), jnp.float32)
            for _ in range(query_rows // query_tile)
        ]

        def one_head(head, sums):
            mine = lane_head == head
            results = []
            for tile in range(query_rows // query_tile):
                query = queries[group, tile * query_tile : (tile + 1) * query_tile, :]
                query = jnp.where(mine, query, jnp.zeros_like(query))
                scores = lax.dot_general(
                    query,
                    keys[group],
                    (((1,), (1,)), ((), ())),
                    preferred_element_type=jnp.float32,
                )
                highest = jnp.max(scores, axis=-1, keepdims=True)
                exps = jnp.exp2((scores - highest).astype(jnp.bfloat16))
                product = jnp.dot(
                    exps, values[group], preferred_element_type=jnp.float32
                )
                result = product[:, :lanes] / product[:, lanes:]
                results.append(jnp.where(mine, result, sums[tile]))
            return tuple(results)

        sums = lax.fori_loop(0, group_heads, one_head, tuple(attended_group), unroll=2)
        for tile in range(query_rows // query_tile):
            attended[tile * query_tile : (tile + 1) * query_tile, pl.ds(
                pl.multiple_of(group * lanes, lanes), lanes
            )] = sums[tile].astype(jnp.bfloat16)
        return carry

    lax.fori_loop(0, groups, one_group, 0)


def attention(patch_rows, gain, weights, query_from, query_rows, head_dim):
    groups, width, triple = weights.shape
    lanes = triple // 3
    rows = patch_rows.shape[0]
    whole = pl.BlockSpec(memory_space=pltpu.VMEM)
    return pl.pallas_call(
        functools.partial(attention_kernel, head_dim, query_rows),
        out_shape=jax.ShapeDtypeStruct((query_rows, groups * lanes), jnp.bfloat16),
        in_specs=[pl.BlockSpec(memory_space=pltpu.SMEM), whole, whole, whole],
        out_specs=whole,
        scratch_shapes=[
            pltpu.VMEM((rows, width), jnp.bfloat16),
            pltpu.VMEM((groups, query_rows, lanes), jnp.bfloat16),
            pltpu.VMEM((groups, rows, lanes), jnp.bfloat16),
            pltpu.VMEM((groups, rows, 2 * lanes), jnp.bfloat16),
        ],
        compiler_params=pltpu.CompilerParams(vmem_limit_bytes=VMEM_BYTES),
        cost_estimate=pl.CostEstimate(
            flops=4 * rows * query_rows * groups * lanes * 16,
            bytes_accessed=4 * rows * width,
            transcendentals=rows * query_rows * groups * 8,
        ),
    )(query_from, patch_rows, gain, weights)


def mlp_kernel(query_from, patch_rows, attended, gain, weights, result):
    groups, _, width_full = weights.shape
    rows = attended.shape[0]
    depth = attended.shape[1] // groups
    hidden_part = (weights.shape[1] - depth) // 2
    proj_weight = [weights[group, :depth, :] for group in range(groups)]
    up_weight = [weights[group, depth : depth + hidden_part, :] for group in range(groups)]
    down_weight = [weights[group, depth + hidden_part :, :] for group in range(groups)]
    start = pl.multiple_of(query_from[0], rows)
    own = patch_rows[pl.ds(start, rows), :].astype(jnp.float32)
    mixed = None
    for group in range(groups):
        term = jnp.dot(
            attended[:, group * depth : (group + 1) * depth],
            proj_weight[group],
            preferred_element_type=jnp.float32,
        ).astype(jnp.bfloat16).astype(jnp.float32)
        mixed = term if mixed is None else mixed + term
    hidden = (own + mixed).astype(jnp.bfloat16).astype(jnp.float32)
    normed = layer_norm(hidden, gain[...])
    total = None
    for group in range(groups):
        expanded = jnp.dot(normed, up_weight[group], preferred_element_type=jnp.float32)
        expanded = (
            0.5 * expanded * (1.0 + lax.erf(expanded * math.sqrt(0.5)))
        ).astype(jnp.bfloat16)
        term = jnp.dot(
            expanded, down_weight[group], preferred_element_type=jnp.float32
        ).astype(jnp.bfloat16).astype(jnp.float32)
        total = term if total is None else total + term
    final = (hidden + total).astype(jnp.bfloat16)
    width = result.shape[2]
    for part in range(result.shape[0]):
        result[part] = final[:, part * width : (part + 1) * width]


def mlp(patch_rows, attended, gain, weights, query_from):
    whole = pl.BlockSpec(memory_space=pltpu.VMEM)
    rows, width = attended.shape
    groups, hidden = weights.shape[0], weights.shape[2]
    return pl.pallas_call(
        mlp_kernel,
        out_shape=jax.ShapeDtypeStruct((groups, rows, width // groups), jnp.bfloat16),
        in_specs=[pl.BlockSpec(memory_space=pltpu.SMEM)] + [whole] * 4,
        out_specs=whole,
        compiler_params=pltpu.CompilerParams(vmem_limit_bytes=VMEM_BYTES),
        cost_estimate=pl.CostEstimate(
            flops=4 * rows * width * hidden * groups,
            bytes_accessed=8 * width * hidden * groups,
            transcendentals=rows * hidden * groups,
        ),
    )(query_from, patch_rows, attended, gain, weights)


def per_device(
    voxel_feats,
    slot_rank,
    curve_order,
    patch_shift,
    qkv_weight,
    proj_weight,
    up_weight,
    down_weight,
    norm_gains,
):
    bricks = lax.axis_size("brick")
    model_parts = lax.axis_size("mp")
    my_index = lax.axis_index("brick")
    part_index = lax.axis_index("mp")
    capacity = voxel_feats.shape[0]
    shard_rows = curve_order.shape[0]
    pair_rows = 3 * (shard_rows // 8)
    width_full = voxel_feats.shape[1]
    width_part = width_full // model_parts
    quarter_rows = shard_rows // model_parts
    head_dim = width_full // HEADS
    offset = patch_shift[0].astype(jnp.uint32)
    latest = capacity - pair_rows

    triple = qkv_weight.shape[1]
    spot = jnp.arange(triple, dtype=jnp.int32)
    kind, within = spot // width_part, spot % width_part
    origin = (within // head_dim) * 3 * head_dim + kind * head_dim + within % head_dim
    shuffle = (spot[:, None] == origin[None, :]).astype(jnp.bfloat16)
    qkv_sorted = jnp.dot(
        qkv_weight, shuffle, preferred_element_type=jnp.float32
    ).astype(jnp.bfloat16)
    qkv_all = lax.all_gather(qkv_sorted, "mp", axis=0)
    mlp_all = lax.all_gather(
        jnp.concatenate([proj_weight, up_weight, down_weight], axis=0), "mp", axis=0
    )

    lane_ids = jnp.arange(4, dtype=jnp.int32)
    lane_targets = wrapped(my_index - (lane_ids - 1), bricks)
    low = lane_targets * shard_rows
    below = slot_rank[:, None] < low[None, :]
    upto = slot_rank[:, None] < (low + shard_rows)[None, :]
    run_starts = jnp.sum(below.astype(jnp.int32), axis=0)
    slab_starts = jnp.minimum(run_starts, latest)
    in_run = jnp.logical_and(upto, jnp.logical_not(below))
    slot_ids = jnp.arange(capacity, dtype=jnp.int32)
    spots = slot_ids[:, None] + (lane_ids * pair_rows - slab_starts)[None, :] + 1
    place = jnp.sum(jnp.where(in_run, spots, 0), axis=1, keepdims=True) - 1

    source_brick = curve_order // capacity
    source_slot = curve_order - source_brick * capacity
    source_lane = wrapped(source_brick - my_index + 1, bricks)
    from_lane = source_lane[:, None] == lane_ids[None, :]
    first_slot = jnp.min(jnp.where(from_lane, source_slot[:, None], latest), axis=0)
    first_of_row = jnp.sum(jnp.where(from_lane, first_slot[None, :], 0), axis=1)
    recv_index = source_lane * pair_rows + source_slot - first_of_row
    empty = jnp.full((PATCH,), -1, jnp.int32)
    index = lax.dynamic_slice_in_dim(
        jnp.concatenate([empty, recv_index, empty]), offset, shard_rows + PATCH, 0
    )

    column = (part_index * width_part).astype(jnp.uint32)
    starts = slab_starts.astype(jnp.uint32)
    slabs = jnp.stack(
        [
            lax.dynamic_slice(voxel_feats, (starts[lane], column), (pair_rows, width_part))
            for lane in range(4)
        ]
    )
    patch_rows = enter(index[:, None], slabs, bricks, model_parts)
    query_from = (lax.rem(part_index * quarter_rows, PATCH))[None]
    attended = attention(
        patch_rows, norm_gains[0:1], qkv_all, query_from, quarter_rows, head_dim
    )
    result = mlp(patch_rows, attended, norm_gains[1:2], mlp_all, query_from)
    return leave(index[None, :], place, result, bricks, 4, pair_rows)


def solution(mesh):
    return jax.shard_map(
        per_device,
        mesh=mesh,
        in_specs=(
            P("brick", None),
            P("brick"),
            P("brick"),
            P(),
            P(None, "mp"),
            P("mp", None),
            P(None, "mp"),
            P("mp", None),
            P(),
        ),
        out_specs=P("brick", "mp"),
        check_vma=False,
    )
```

```python
import functools
import math

import jax
import jax.numpy as jnp
from jax import lax
from jax.experimental import pallas as pl
from jax.experimental.pallas import tpu as pltpu
from jax.sharding import PartitionSpec as P

HEADS = 32
PATCH = 1024
EPSILON = 1e-05
ALIGN = 16
VMEM_BYTES = 56 * 1024 * 1024


MESH = pl.DeviceIdType.MESH


def gathered(value, reach):
    parts = lax.axis_size("mp")
    half = parts // 2
    if reach == "far":
        groups = [[first, first + half] for first in range(half)]
    else:
        groups = [list(range(half)), list(range(half, parts))]
    return lax.all_gather(value, "mp", axis=0, tiled=True, axis_index_groups=groups)


def wrapped(value, count):
    value = jnp.where(value < 0, value + count, value)
    return jnp.where(value >= count, value - count, value)


def greet_all(bricks, parts):
    brick, part = lax.axis_index("brick"), lax.axis_index("mp")
    barrier = pltpu.get_barrier_semaphore()
    peers = [(0, step) for step in range(1, parts)]
    peers += [(away, step) for away in (-1, 1) for step in range(parts)]
    peers += [(-2, 0), (2, 0)]
    for away, step in peers:
        pl.semaphore_signal(
            barrier,
            inc=1,
            device_id=(lax.rem(brick + away + bricks, bricks), lax.rem(part + step, parts)),
            device_id_type=MESH,
        )
    pl.semaphore_wait(barrier, len(peers))


def enter_kernel(
    bricks,
    parts,
    index,
    slabs,
    patch_rows,
    arrived,
    total,
    merged,
    window_in,
    head_in,
    column_index,
    lane_send,
    lane_recv,
    window_send,
    window_recv,
    head_send,
    head_recv,
):
    brick, part = lax.axis_index("brick"), lax.axis_index("mp")
    slab_rows, width = slabs.shape[1], slabs.shape[2]
    rows = index.shape[1]
    tile = 1024
    lane_width = column_index.shape[1]
    quarter = (rows - PATCH) // parts
    greet_all(bricks, parts)

    def lane_copy(lane):
        return pltpu.make_async_remote_copy(
            src_ref=slabs.at[lane],
            dst_ref=arrived.at[lane],
            send_sem=lane_send.at[lane],
            recv_sem=lane_recv.at[lane],
            device_id=(lax.rem(brick - lane + 1 + bricks, bricks), part),
            device_id_type=MESH,
        )

    for lane in (3, 0, 2):
        lane_copy(lane).start()
    for start in range(0, rows, tile):
        column_index[start : start + tile, :] = jnp.broadcast_to(
            index[:, start : start + tile], (lane_width, tile)
        ).T

    def merge(lane, source, first):
        def one_tile(step, carry):
            at = pl.ds(pl.multiple_of(step * tile, tile), tile)
            mine = column_index[at, :] - lane * slab_rows
            spots = lax.broadcasted_iota(jnp.int32, (tile, lane_width), 1)
            chosen = jnp.concatenate(
                [
                    jnp.where(mine == spots + start, 1.0, 0.0).astype(jnp.bfloat16)
                    for start in range(0, slab_rows, lane_width)
                ],
                axis=1,
            )
            term = jnp.dot(chosen, source, preferred_element_type=jnp.float32)
            if first:
                total[at, :] = term
            else:
                total[at, :] += term
            return carry

        lax.fori_loop(0, rows // tile, one_tile, 0)

    merge(1, slabs[1], True)
    for lane in (2, 0, 3):
        lane_copy(lane).wait()
        merge(lane, arrived[lane], False)
    merged[...] = total[...].astype(jnp.bfloat16)

    def patch_start(target):
        return pl.multiple_of((target * quarter // PATCH + 1) * PATCH, PATCH)

    last = rows - PATCH

    def head_copy(step):
        target = lax.rem(part + step, parts)
        return pltpu.make_async_remote_copy(
            src_ref=merged.at[pl.ds(0, PATCH)],
            dst_ref=head_in.at[step],
            send_sem=head_send.at[step],
            recv_sem=head_recv.at[step],
            device_id=(lax.rem(brick - 1 + bricks, bricks), target),
            device_id_type=MESH,
        )

    def window_copy(step):
        target = lax.rem(part + step, parts)
        return pltpu.make_async_remote_copy(
            src_ref=merged.at[pl.ds(patch_start(target), PATCH)],
            dst_ref=window_in.at[step],
            send_sem=window_send.at[step],
            recv_sem=window_recv.at[step],
            device_id=(brick, target),
            device_id_type=MESH,
        )

    for step in range(parts):

        @pl.when(patch_start(lax.rem(part + step, parts)) == last)
        def _():
            head_copy(step).start()

    for step in range(1, parts):
        window_copy(step).start()

    def columns(step):
        source = lax.rem(part - step + parts, parts)
        return pl.ds(pl.multiple_of(source * width, width), width)

    patch_rows[:, columns(0)] = merged[pl.ds(patch_start(part), PATCH), :]
    for step in range(1, parts):
        window_copy(step).wait()
        patch_rows[:, columns(step)] = window_in[step]

    @pl.when(patch_start(part) == last)
    def _():
        for step in range(parts):
            head_copy(step).wait_recv()
            patch_rows[:, columns(step)] += head_in[step]

    for step in range(parts):

        @pl.when(patch_start(lax.rem(part + step, parts)) == last)
        def _():
            head_copy(step).wait_send()


def enter(index, slabs, bricks, parts):
    lanes, slab_rows, width = slabs.shape
    rows = index.shape[1]
    whole = pl.BlockSpec(memory_space=pltpu.VMEM)
    return pl.pallas_call(
        functools.partial(enter_kernel, bricks, parts),
        out_shape=jax.ShapeDtypeStruct((PATCH, width * parts), jnp.bfloat16),
        in_specs=[whole, whole],
        out_specs=whole,
        scratch_shapes=[
            pltpu.VMEM((lanes, slab_rows, width), jnp.bfloat16),
            pltpu.VMEM((rows, width), jnp.float32),
            pltpu.VMEM((rows, width), jnp.bfloat16),
            pltpu.VMEM((parts, PATCH, width), jnp.bfloat16),
            pltpu.VMEM((parts, PATCH, width), jnp.bfloat16),
            pltpu.VMEM((rows, 128), jnp.int32),
            pltpu.SemaphoreType.DMA((lanes,)),
            pltpu.SemaphoreType.DMA((lanes,)),
            pltpu.SemaphoreType.DMA((parts,)),
            pltpu.SemaphoreType.DMA((parts,)),
            pltpu.SemaphoreType.DMA((parts,)),
            pltpu.SemaphoreType.DMA((parts,)),
        ],
        compiler_params=pltpu.CompilerParams(
            collective_id=0, has_side_effects=True, vmem_limit_bytes=VMEM_BYTES
        ),
        cost_estimate=pl.CostEstimate(
            flops=2 * rows * lanes * slab_rows * width,
            bytes_accessed=20 * slab_rows * width * lanes,
            transcendentals=0,
        ),
    )(index, slabs)


def leave_kernel(
    bricks,
    parts,
    index,
    result,
    arrived,
    rows_in,
    leaving,
    window_send,
    window_recv,
    tail_send,
    tail_recv,
    lane_send,
    lane_recv,
):
    brick, part = lax.axis_index("brick"), lax.axis_index("mp")
    lanes, slab_rows, width = leaving.shape
    quarter = result.shape[1]
    rows = rows_in.shape[0]
    last = rows - PATCH
    greet_all(bricks, parts)

    def row_start(source):
        return PATCH + source * quarter

    def tail_copy(step):
        target = lax.rem(part + step, parts)
        start = pl.multiple_of(jnp.maximum(row_start(part) - last, 0), quarter)
        return pltpu.make_async_remote_copy(
            src_ref=result.at[target],
            dst_ref=rows_in.at[pl.ds(start, quarter)],
            send_sem=tail_send.at[step],
            recv_sem=tail_recv.at[part],
            device_id=(lax.rem(brick + 1, bricks), target),
            device_id_type=MESH,
        )

    def window_copy(step):
        target = lax.rem(part + step, parts)
        start = pl.multiple_of(row_start(part), quarter)
        return pltpu.make_async_remote_copy(
            src_ref=result.at[target],
            dst_ref=rows_in.at[pl.ds(start, quarter)],
            send_sem=window_send.at[step],
            recv_sem=window_recv.at[step],
            device_id=(brick, target),
            device_id_type=MESH,
        )

    def tail_arrival(source):
        return pltpu.make_async_remote_copy(
            src_ref=result.at[0],
            dst_ref=rows_in.at[pl.ds(row_start(source) - last, quarter)],
            send_sem=tail_send.at[0],
            recv_sem=tail_recv.at[source],
            device_id=(lax.rem(brick + 1, bricks), part),
            device_id_type=MESH,
        )

    def window_arrival(step):
        source = lax.rem(part - step + parts, parts)
        return pltpu.make_async_remote_copy(
            src_ref=result.at[0],
            dst_ref=rows_in.at[pl.ds(pl.multiple_of(row_start(source), quarter), quarter)],
            send_sem=window_send.at[step],
            recv_sem=window_recv.at[step],
            device_id=(brick, source),
            device_id_type=MESH,
        )

    sends_tail = row_start(part) >= last

    @pl.when(sends_tail)
    def _():
        for step in range(parts):
            tail_copy(step).start()

    for step in range(1, parts):
        window_copy(step).start()
    rows_in[pl.ds(pl.multiple_of(row_start(part), quarter), quarter), :] = result[part]
    for step in range(1, parts):
        window_arrival(step).wait_recv()
    for source in range(parts):
        if row_start(source) >= last:
            tail_arrival(source).wait_recv()

    def lane_copy(lane):
        return pltpu.make_async_remote_copy(
            src_ref=leaving.at[lane],
            dst_ref=arrived.at[lane],
            send_sem=lane_send.at[lane],
            recv_sem=lane_recv.at[lane],
            device_id=(lax.rem(brick + lane - 1 + bricks, bricks), part),
            device_id_type=MESH,
        )

    def spread(lane):
        spots = lax.broadcasted_iota(jnp.int32, (slab_rows, rows), 0) + lane * slab_rows
        chosen = jnp.where(index[...] == spots, 1.0, 0.0).astype(jnp.bfloat16)
        return jnp.dot(
            chosen, rows_in[...], preferred_element_type=jnp.float32
        ).astype(jnp.bfloat16)

    for lane in (3, 0, 2):
        leaving[lane] = spread(lane)
        lane_copy(lane).start()
    arrived[1] = spread(1)
    for lane in (2, 0, 3):
        lane_copy(lane).wait()

    for step in range(1, parts):
        window_copy(step).wait_send()

    @pl.when(sends_tail)
    def _():
        for step in range(parts):
            tail_copy(step).wait_send()


def leave(index, result, bricks, lanes, slab_rows):
    parts, quarter, width = result.shape
    rows = index.shape[1]
    whole = pl.BlockSpec(memory_space=pltpu.VMEM)
    return pl.pallas_call(
        functools.partial(leave_kernel, bricks, parts),
        out_shape=jax.ShapeDtypeStruct((lanes, slab_rows, width), jnp.bfloat16),
        in_specs=[whole, whole],
        out_specs=whole,
        scratch_shapes=[
            pltpu.VMEM((rows, width), jnp.bfloat16),
            pltpu.VMEM((lanes, slab_rows, width), jnp.bfloat16),
            pltpu.SemaphoreType.DMA((parts,)),
            pltpu.SemaphoreType.DMA((parts,)),
            pltpu.SemaphoreType.DMA((parts,)),
            pltpu.SemaphoreType.DMA((parts,)),
            pltpu.SemaphoreType.DMA((lanes,)),
            pltpu.SemaphoreType.DMA((lanes,)),
        ],
        compiler_params=pltpu.CompilerParams(
            collective_id=1, has_side_effects=True, vmem_limit_bytes=VMEM_BYTES
        ),
        cost_estimate=pl.CostEstimate(
            flops=2 * rows * lanes * slab_rows * width,
            bytes_accessed=20 * slab_rows * width * lanes,
            transcendentals=0,
        ),
    )(index, result)


def cut_kernel(starts, voxel_feats, slabs, held, arrived):
    part = lax.axis_index("mp")
    lanes, slab_rows, width = slabs.shape
    held_rows = held.shape[1]

    def copy(lane):
        first = pl.multiple_of(starts[1, lane], ALIGN)
        column = pl.multiple_of(part * width, width)
        return pltpu.make_async_copy(
            voxel_feats.at[pl.ds(first, held_rows), pl.ds(column, width)],
            held.at[lane],
            arrived.at[lane],
        )

    for lane in range(lanes):
        copy(lane).start()
    for lane in range(lanes):
        copy(lane).wait()
        rows = held[lane].astype(jnp.float32)
        ahead = starts[0, lane] - starts[1, lane]
        turned = pltpu.roll(rows, lax.rem(held_rows - ahead, held_rows), 0)
        slabs[lane] = turned[:slab_rows].astype(jnp.bfloat16)


def cut(starts, voxel_feats, slab_rows, parts):
    lanes = starts.shape[1]
    width = voxel_feats.shape[1] // parts
    return pl.pallas_call(
        cut_kernel,
        out_shape=jax.ShapeDtypeStruct((lanes, slab_rows, width), jnp.bfloat16),
        in_specs=[pl.BlockSpec(memory_space=pltpu.SMEM), pl.BlockSpec(memory_space=pl.ANY)],
        out_specs=pl.BlockSpec(memory_space=pltpu.VMEM),
        scratch_shapes=[
            pltpu.VMEM((lanes, slab_rows + ALIGN, width), jnp.bfloat16),
            pltpu.SemaphoreType.DMA((lanes,)),
        ],
        compiler_params=pltpu.CompilerParams(vmem_limit_bytes=VMEM_BYTES),
    )(starts, voxel_feats)


def place_kernel(starts, slabs, out, total):
    lanes, slab_rows, width = slabs.shape
    total[...] = jnp.zeros_like(total)
    for lane in range(lanes):
        rows = jnp.concatenate(
            [slabs[lane].astype(jnp.float32), jnp.zeros((ALIGN, width), jnp.float32)], axis=0
        )
        turned = pltpu.roll(rows, starts[0, lane] - starts[1, lane], 0)
        at = pl.ds(pl.multiple_of(starts[1, lane], ALIGN), slab_rows + ALIGN)
        total[at, :] += turned
    out[...] = total[...].astype(jnp.bfloat16)


def place(starts, slabs, capacity):
    width = slabs.shape[2]
    whole = pl.BlockSpec(memory_space=pltpu.VMEM)
    return pl.pallas_call(
        place_kernel,
        out_shape=jax.ShapeDtypeStruct((capacity, width), jnp.bfloat16),
        in_specs=[pl.BlockSpec(memory_space=pltpu.SMEM), whole],
        out_specs=whole,
        scratch_shapes=[pltpu.VMEM((capacity, width), jnp.float32)],
        compiler_params=pltpu.CompilerParams(vmem_limit_bytes=VMEM_BYTES),
    )(starts, slabs)


def layer_norm(values, gain):
    centred = values - jnp.mean(values, axis=-1, keepdims=True)
    spread = jnp.mean(centred * centred, axis=-1, keepdims=True)
    return (centred * lax.rsqrt(spread + EPSILON) * gain).astype(jnp.bfloat16)


def attention_kernel(
    head_dim,
    query_tile,
    query_from,
    patch_rows,
    gain,
    weights,
    attended,
    normed,
    queries,
    keys,
    values,
    held,
    arrived,
):
    groups, _, triple = weights.shape

    def copy(group):
        return pltpu.make_async_copy(weights.at[group], held.at[group], arrived.at[group])

    for group in range(groups):
        copy(group).start()
    lanes = triple // 3
    group_heads = lanes // head_dim
    query_rows = attended.shape[0]
    normed[...] = layer_norm(patch_rows[...].astype(jnp.float32), gain[...])
    start = pl.multiple_of(query_from[0], query_rows)
    scale = head_dim ** (-0.5) * math.log2(math.e)
    lane_head = lax.broadcasted_iota(jnp.int32, (1, lanes), 1) // head_dim
    for group in range(groups):
        copy(group).wait()
        weight = held[group]
        queries[group] = (
            jnp.dot(
                normed[pl.ds(start, query_rows), :],
                weight[:, :lanes],
                preferred_element_type=jnp.float32,
            )
            * scale
        ).astype(jnp.bfloat16)
        both = jnp.dot(
            normed[...], weight[:, lanes:], preferred_element_type=jnp.float32
        ).astype(jnp.bfloat16)
        keys[group] = both[:, :lanes]
        values[group, :, :lanes] = both[:, lanes:]
        values[group, :, lanes:] = jnp.ones_like(both[:, lanes:])

    def one_group(group, carry):
        attended_group = [
            jnp.zeros((query_tile, lanes), jnp.float32)
            for _ in range(query_rows // query_tile)
        ]

        def one_head(head, sums):
            mine = lane_head == head
            results = []
            for tile in range(query_rows // query_tile):
                query = queries[group, tile * query_tile : (tile + 1) * query_tile, :]
                query = jnp.where(mine, query, jnp.zeros_like(query))
                scores = lax.dot_general(
                    query,
                    keys[group],
                    (((1,), (1,)), ((), ())),
                    preferred_element_type=jnp.float32,
                )
                highest = jnp.max(scores, axis=-1, keepdims=True)
                exps = jnp.exp2((scores - highest).astype(jnp.bfloat16))
                product = jnp.dot(
                    exps, values[group], preferred_element_type=jnp.float32
                )
                result = product[:, :lanes] / product[:, lanes:]
                results.append(jnp.where(mine, result, sums[tile]))
            return tuple(results)

        sums = lax.fori_loop(0, group_heads, one_head, tuple(attended_group), unroll=2)
        for tile in range(query_rows // query_tile):
            attended[tile * query_tile : (tile + 1) * query_tile, pl.ds(
                pl.multiple_of(group * lanes, lanes), lanes
            )] = sums[tile].astype(jnp.bfloat16)
        return carry

    lax.fori_loop(0, groups, one_group, 0)


def attention(patch_rows, gain, weights, query_from, query_rows, head_dim):
    groups, width, triple = weights.shape
    lanes = triple // 3
    rows = patch_rows.shape[0]
    whole = pl.BlockSpec(memory_space=pltpu.VMEM)
    return pl.pallas_call(
        functools.partial(attention_kernel, head_dim, query_rows),
        out_shape=jax.ShapeDtypeStruct((query_rows, groups * lanes), jnp.bfloat16),
        in_specs=[
            pl.BlockSpec(memory_space=pltpu.SMEM),
            whole,
            whole,
            pl.BlockSpec(memory_space=pl.ANY),
        ],
        out_specs=whole,
        scratch_shapes=[
            pltpu.VMEM((rows, width), jnp.bfloat16),
            pltpu.VMEM((groups, query_rows, lanes), jnp.bfloat16),
            pltpu.VMEM((groups, rows, lanes), jnp.bfloat16),
            pltpu.VMEM((groups, rows, 2 * lanes), jnp.bfloat16),
            pltpu.VMEM(weights.shape, jnp.bfloat16),
            pltpu.SemaphoreType.DMA((groups,)),
        ],
        compiler_params=pltpu.CompilerParams(vmem_limit_bytes=VMEM_BYTES),
        cost_estimate=pl.CostEstimate(
            flops=4 * rows * query_rows * groups * lanes * 16,
            bytes_accessed=4 * rows * width,
            transcendentals=rows * query_rows * groups * 8,
        ),
    )(query_from, patch_rows, gain, weights)


def mlp_kernel(query_from, patch_rows, attended, gain, weights, result):
    groups, _, width_full = weights.shape
    rows = attended.shape[0]
    depth = attended.shape[1] // groups
    hidden_part = (weights.shape[1] - depth) // 2
    proj_weight = [weights[group, :depth, :] for group in range(groups)]
    up_weight = [weights[group, depth : depth + hidden_part, :] for group in range(groups)]
    down_weight = [weights[group, depth + hidden_part :, :] for group in range(groups)]
    start = pl.multiple_of(query_from[0], rows)
    own = patch_rows[pl.ds(start, rows), :].astype(jnp.float32)
    mixed = None
    for group in range(groups):
        term = jnp.dot(
            attended[:, group * depth : (group + 1) * depth],
            proj_weight[group],
            preferred_element_type=jnp.float32,
        ).astype(jnp.bfloat16).astype(jnp.float32)
        mixed = term if mixed is None else mixed + term
    hidden = (own + mixed).astype(jnp.bfloat16).astype(jnp.float32)
    normed = layer_norm(hidden, gain[...])
    total = None
    for group in range(groups):
        expanded = jnp.dot(normed, up_weight[group], preferred_element_type=jnp.float32)
        expanded = (
            0.5 * expanded * (1.0 + lax.erf(expanded * math.sqrt(0.5)))
        ).astype(jnp.bfloat16)
        term = jnp.dot(
            expanded, down_weight[group], preferred_element_type=jnp.float32
        ).astype(jnp.bfloat16).astype(jnp.float32)
        total = term if total is None else total + term
    final = (hidden + total).astype(jnp.bfloat16)
    width = result.shape[2]
    for part in range(result.shape[0]):
        result[part] = final[:, part * width : (part + 1) * width]


def mlp(patch_rows, attended, gain, weights, query_from):
    whole = pl.BlockSpec(memory_space=pltpu.VMEM)
    rows, width = attended.shape
    groups, hidden = weights.shape[0], weights.shape[2]
    return pl.pallas_call(
        mlp_kernel,
        out_shape=jax.ShapeDtypeStruct((groups, rows, width // groups), jnp.bfloat16),
        in_specs=[pl.BlockSpec(memory_space=pltpu.SMEM)] + [whole] * 4,
        out_specs=whole,
        compiler_params=pltpu.CompilerParams(vmem_limit_bytes=VMEM_BYTES),
        cost_estimate=pl.CostEstimate(
            flops=4 * rows * width * hidden * groups,
            bytes_accessed=8 * width * hidden * groups,
            transcendentals=rows * hidden * groups,
        ),
    )(query_from, patch_rows, attended, gain, weights)


def per_device(
    voxel_feats,
    slot_rank,
    curve_order,
    patch_shift,
    qkv_weight,
    proj_weight,
    up_weight,
    down_weight,
    norm_gains,
):
    bricks = lax.axis_size("brick")
    model_parts = lax.axis_size("mp")
    my_index = lax.axis_index("brick")
    part_index = lax.axis_index("mp")
    capacity = voxel_feats.shape[0]
    shard_rows = curve_order.shape[0]
    pair_rows = 3 * (shard_rows // 8)
    width_full = voxel_feats.shape[1]
    width_part = width_full // model_parts
    quarter_rows = shard_rows // model_parts
    head_dim = width_full // HEADS
    offset = patch_shift[0].astype(jnp.uint32)
    latest = capacity - pair_rows

    triple = qkv_weight.shape[1]
    spot = jnp.arange(triple, dtype=jnp.int32)
    kind, within = spot // width_part, spot % width_part
    origin = (within // head_dim) * 3 * head_dim + kind * head_dim + within % head_dim
    shuffle = (spot[:, None] == origin[None, :]).astype(jnp.bfloat16)
    qkv_sorted = jnp.dot(
        qkv_weight, shuffle, preferred_element_type=jnp.float32
    ).astype(jnp.bfloat16)
    qkv_half = gathered(qkv_sorted[None], "far")
    mlp_half = gathered(
        jnp.concatenate([proj_weight, up_weight, down_weight], axis=0)[None], "far"
    )

    lane_ids = jnp.arange(4, dtype=jnp.int32)
    lane_targets = wrapped(my_index - (lane_ids - 1), bricks)
    low = lane_targets * shard_rows
    below = slot_rank[:, None] < low[None, :]
    run_starts = jnp.sum(below.astype(jnp.int32), axis=0)
    slab_starts = jnp.minimum(run_starts, latest)
    aligned = jnp.minimum(slab_starts // ALIGN * ALIGN, latest - ALIGN)
    starts = jnp.stack([slab_starts, aligned])

    source_brick = curve_order // capacity
    source_slot = curve_order - source_brick * capacity
    source_lane = wrapped(source_brick - my_index + 1, bricks)
    from_lane = source_lane[:, None] == lane_ids[None, :]
    first_slot = jnp.min(jnp.where(from_lane, source_slot[:, None], latest), axis=0)
    first_of_row = jnp.sum(jnp.where(from_lane, first_slot[None, :], 0), axis=1)
    recv_index = source_lane * pair_rows + source_slot - first_of_row
    empty = jnp.full((PATCH,), -1, jnp.int32)
    index = lax.dynamic_slice_in_dim(
        jnp.concatenate([empty, recv_index, empty]), offset, shard_rows + PATCH, 0
    )

    slabs = cut(starts, voxel_feats, pair_rows, model_parts)
    qkv_half, slabs = lax.optimization_barrier((qkv_half, slabs))
    qkv_all = gathered(qkv_half, "near")
    patch_rows = enter(index[None, :], slabs, bricks, model_parts)
    mlp_half, patch_rows = lax.optimization_barrier((mlp_half, patch_rows))
    mlp_all = gathered(mlp_half, "near")
    query_from = (lax.rem(part_index * quarter_rows, PATCH))[None]
    attended = attention(
        patch_rows, norm_gains[0:1], qkv_all, query_from, quarter_rows, head_dim
    )
    result = mlp(patch_rows, attended, norm_gains[1:2], mlp_all, query_from)
    returned = leave(index[None, :], result, bricks, 4, pair_rows)
    return place(starts, returned, capacity)


def solution(mesh):
    return jax.shard_map(
        per_device,
        mesh=mesh,
        in_specs=(
            P("brick", None),
            P("brick"),
            P("brick"),
            P(),
            P(None, "mp"),
            P("mp", None),
            P(None, "mp"),
            P("mp", None),
            P(),
        ),
        out_specs=P("brick", "mp"),
        check_vma=False,
    )
```

```python
import functools
import math

import jax
import jax.numpy as jnp
from jax import lax
from jax.experimental import pallas as pl
from jax.experimental.pallas import tpu as pltpu
from jax.sharding import PartitionSpec as P

HEADS = 32
PATCH = 1024
EPSILON = 1e-05
ALIGN = 16
VMEM_BYTES = 56 * 1024 * 1024


MESH = pl.DeviceIdType.MESH


def passed(value, patches, patch_step, near_step):
    parts = lax.axis_size("mp")
    half = parts // patches
    pairs = []
    for source in range(parts):
        patch, place = source // half, source % half
        target = (patch + patch_step) % patches * half + (place + near_step) % half
        pairs.append((source, target))
    return lax.ppermute(value, "mp", pairs)


def wrapped(value, count):
    value = jnp.where(value < 0, value + count, value)
    return jnp.where(value >= count, value - count, value)


def greet_all(bricks, parts, wide):
    brick, part = lax.axis_index("brick"), lax.axis_index("mp")
    barrier = pltpu.get_barrier_semaphore()
    peers = [(0, step) for step in range(1, parts)]
    peers += [(away, step) for away in (-1, 1) for step in range(parts if wide else 1)]
    peers += [(-2, 0), (2, 0)]
    for away, step in peers:
        pl.semaphore_signal(
            barrier,
            inc=1,
            device_id=(lax.rem(brick + away + bricks, bricks), lax.rem(part + step, parts)),
            device_id_type=MESH,
        )
    pl.semaphore_wait(barrier, len(peers))


def enter_kernel(
    bricks,
    parts,
    index,
    slabs,
    patch_rows,
    arrived,
    total,
    merged,
    window_in,
    head_in,
    column_index,
    lane_send,
    lane_recv,
    far_send,
    far_recv,
    near_send,
    near_recv,
    head_send,
    head_recv,
):
    brick, part = lax.axis_index("brick"), lax.axis_index("mp")
    slab_rows, width = slabs.shape[1], slabs.shape[2]
    rows = index.shape[1]
    tile = 1024
    lane_width = column_index.shape[1]
    greet_all(bricks, parts, False)

    def lane_copy(lane):
        return pltpu.make_async_remote_copy(
            src_ref=slabs.at[lane],
            dst_ref=arrived.at[lane],
            send_sem=lane_send.at[lane],
            recv_sem=lane_recv.at[lane],
            device_id=(lax.rem(brick - lane + 1 + bricks, bricks), part),
            device_id_type=MESH,
        )

    for lane in (3, 0, 2):
        lane_copy(lane).start()
    for start in range(0, rows, tile):
        column_index[start : start + tile, :] = jnp.broadcast_to(
            index[:, start : start + tile], (lane_width, tile)
        ).T

    def merge(lane, source, first):
        def one_tile(step, carry):
            at = pl.ds(pl.multiple_of(step * tile, tile), tile)
            mine = column_index[at, :] - lane * slab_rows
            spots = lax.broadcasted_iota(jnp.int32, (tile, lane_width), 1)
            chosen = jnp.concatenate(
                [
                    jnp.where(mine == spots + start, 1.0, 0.0).astype(jnp.bfloat16)
                    for start in range(0, slab_rows, lane_width)
                ],
                axis=1,
            )
            term = jnp.dot(chosen, source, preferred_element_type=jnp.float32)
            if first:
                total[at, :] = term
            else:
                total[at, :] += term
            return carry

        lax.fori_loop(0, rows // tile, one_tile, 0)

    merge(1, slabs[1], True)
    for lane in (2, 0, 3):
        lane_copy(lane).wait()
        merge(lane, arrived[lane], False)
    merged[...] = total[...].astype(jnp.bfloat16)

    patches = (rows - PATCH) // PATCH
    half = parts // patches
    patch, place = part // half, lax.rem(part, half)
    last = patches - 1

    def rows_of(which):
        return pl.ds(pl.multiple_of((which + 1) * PATCH, PATCH), PATCH)

    head_copy = pltpu.make_async_remote_copy(
        src_ref=merged.at[pl.ds(0, PATCH)],
        dst_ref=head_in,
        send_sem=head_send.at[0],
        recv_sem=head_recv.at[0],
        device_id=(lax.rem(brick - 1 + bricks, bricks), part),
        device_id_type=MESH,
    )
    head_copy.start()

    def far_target(step):
        return lax.rem(patch + step, patches)

    def far_copy(step):
        return pltpu.make_async_remote_copy(
            src_ref=merged.at[rows_of(far_target(step))],
            dst_ref=window_in.at[part],
            send_sem=far_send.at[step],
            recv_sem=far_recv.at[step],
            device_id=(brick, far_target(step) * half + place),
            device_id_type=MESH,
        )

    def near_copy(step, far_step):
        source = lax.rem(patch - far_step + patches, patches) * half + place
        return pltpu.make_async_remote_copy(
            src_ref=window_in.at[source],
            dst_ref=window_in.at[source],
            send_sem=near_send.at[step, far_step],
            recv_sem=near_recv.at[step, far_step],
            device_id=(brick, patch * half + lax.rem(place + step, half)),
            device_id_type=MESH,
        )

    def start_far(late):
        for step in range(1, patches):

            @pl.when((far_target(step) == last) if late else (far_target(step) != last))
            def _():
                far_copy(step).start()

    def start_own():
        window_in[part] = merged[rows_of(patch), :]
        for step in range(1, half):
            near_copy(step, 0).start()

    start_far(False)

    @pl.when(patch != last)
    def _():
        start_own()

    head_copy.wait_recv()
    merged[rows - PATCH :, :] += head_in[...]
    start_far(True)

    @pl.when(patch == last)
    def _():
        start_own()

    for far_step in range(1, patches):
        far_copy(far_step).wait()
        for step in range(1, half):
            near_copy(step, far_step).start()
    for far_step in range(patches):
        for step in range(1, half):
            near_copy(step, far_step).wait()
    head_copy.wait_send()
    for source in range(parts):
        patch_rows[:, source * width : (source + 1) * width] = window_in[source]


def enter(index, slabs, bricks, parts):
    lanes, slab_rows, width = slabs.shape
    rows = index.shape[1]
    whole = pl.BlockSpec(memory_space=pltpu.VMEM)
    return pl.pallas_call(
        functools.partial(enter_kernel, bricks, parts),
        out_shape=jax.ShapeDtypeStruct((PATCH, width * parts), jnp.bfloat16),
        in_specs=[whole, whole],
        out_specs=whole,
        scratch_shapes=[
            pltpu.VMEM((lanes, slab_rows, width), jnp.bfloat16),
            pltpu.VMEM((rows, width), jnp.float32),
            pltpu.VMEM((rows, width), jnp.bfloat16),
            pltpu.VMEM((parts, PATCH, width), jnp.bfloat16),
            pltpu.VMEM((PATCH, width), jnp.bfloat16),
            pltpu.VMEM((rows, 128), jnp.int32),
            pltpu.SemaphoreType.DMA((lanes,)),
            pltpu.SemaphoreType.DMA((lanes,)),
            pltpu.SemaphoreType.DMA((parts,)),
            pltpu.SemaphoreType.DMA((parts,)),
            pltpu.SemaphoreType.DMA((parts, parts)),
            pltpu.SemaphoreType.DMA((parts, parts)),
            pltpu.SemaphoreType.DMA((1,)),
            pltpu.SemaphoreType.DMA((1,)),
        ],
        compiler_params=pltpu.CompilerParams(
            collective_id=0, has_side_effects=True, vmem_limit_bytes=VMEM_BYTES
        ),
        cost_estimate=pl.CostEstimate(
            flops=2 * rows * lanes * slab_rows * width,
            bytes_accessed=20 * slab_rows * width * lanes,
            transcendentals=0,
        ),
    )(index, slabs)


def leave_kernel(
    bricks,
    parts,
    index,
    result,
    arrived,
    rows_in,
    leaving,
    total,
    window_send,
    window_recv,
    tail_send,
    tail_recv,
    lane_send,
    lane_recv,
):
    brick, part = lax.axis_index("brick"), lax.axis_index("mp")
    lanes, slab_rows, width = leaving.shape
    quarter = result.shape[1]
    rows = rows_in.shape[0]
    last = rows - PATCH
    greet_all(bricks, parts, True)

    def row_start(source):
        return PATCH + source * quarter

    def tail_copy(step):
        target = lax.rem(part + step, parts)
        start = pl.multiple_of(jnp.maximum(row_start(part) - last, 0), quarter)
        return pltpu.make_async_remote_copy(
            src_ref=result.at[target],
            dst_ref=rows_in.at[pl.ds(start, quarter)],
            send_sem=tail_send.at[step],
            recv_sem=tail_recv.at[part],
            device_id=(lax.rem(brick + 1, bricks), target),
            device_id_type=MESH,
        )

    def window_copy(step):
        target = lax.rem(part + step, parts)
        start = pl.multiple_of(row_start(part), quarter)
        return pltpu.make_async_remote_copy(
            src_ref=result.at[target],
            dst_ref=rows_in.at[pl.ds(start, quarter)],
            send_sem=window_send.at[step],
            recv_sem=window_recv.at[step],
            device_id=(brick, target),
            device_id_type=MESH,
        )

    def tail_arrival(source):
        return pltpu.make_async_remote_copy(
            src_ref=result.at[0],
            dst_ref=rows_in.at[pl.ds(row_start(source) - last, quarter)],
            send_sem=tail_send.at[0],
            recv_sem=tail_recv.at[source],
            device_id=(lax.rem(brick + 1, bricks), part),
            device_id_type=MESH,
        )

    def window_arrival(step):
        source = lax.rem(part - step + parts, parts)
        return pltpu.make_async_remote_copy(
            src_ref=result.at[0],
            dst_ref=rows_in.at[pl.ds(pl.multiple_of(row_start(source), quarter), quarter)],
            send_sem=window_send.at[step],
            recv_sem=window_recv.at[step],
            device_id=(brick, source),
            device_id_type=MESH,
        )

    sends_tail = row_start(part) >= last

    @pl.when(sends_tail)
    def _():
        for step in range(parts):
            tail_copy(step).start()

    for step in range(1, parts):
        window_copy(step).start()
    rows_in[pl.ds(pl.multiple_of(row_start(part), quarter), quarter), :] = result[part]
    for step in range(1, parts):
        window_arrival(step).wait_recv()
    def lane_copy(lane):
        return pltpu.make_async_remote_copy(
            src_ref=leaving.at[lane],
            dst_ref=arrived.at[lane],
            send_sem=lane_send.at[lane],
            recv_sem=lane_recv.at[lane],
            device_id=(lax.rem(brick + lane - 1 + bricks, bricks), part),
            device_id_type=MESH,
        )

    def spread(lane, start, stop):
        spots = lax.broadcasted_iota(jnp.int32, (slab_rows, stop - start), 0)
        chosen = jnp.where(
            index[:, start:stop] == spots + lane * slab_rows, 1.0, 0.0
        ).astype(jnp.bfloat16)
        return jnp.dot(chosen, rows_in[start:stop, :], preferred_element_type=jnp.float32)

    for lane in range(lanes):
        total[lane] = spread(lane, PATCH, rows)
    for source in range(parts):
        if row_start(source) >= last:
            tail_arrival(source).wait_recv()
    for lane in (3, 0, 2):
        leaving[lane] = (total[lane] + spread(lane, 0, PATCH)).astype(jnp.bfloat16)
        lane_copy(lane).start()
    arrived[1] = (total[1] + spread(1, 0, PATCH)).astype(jnp.bfloat16)
    for lane in (2, 0, 3):
        lane_copy(lane).wait()

    for step in range(1, parts):
        window_copy(step).wait_send()

    @pl.when(sends_tail)
    def _():
        for step in range(parts):
            tail_copy(step).wait_send()


def leave(index, result, bricks, lanes, slab_rows):
    parts, quarter, width = result.shape
    rows = index.shape[1]
    whole = pl.BlockSpec(memory_space=pltpu.VMEM)
    return pl.pallas_call(
        functools.partial(leave_kernel, bricks, parts),
        out_shape=jax.ShapeDtypeStruct((lanes, slab_rows, width), jnp.bfloat16),
        in_specs=[whole, whole],
        out_specs=whole,
        scratch_shapes=[
            pltpu.VMEM((rows, width), jnp.bfloat16),
            pltpu.VMEM((lanes, slab_rows, width), jnp.bfloat16),
            pltpu.VMEM((lanes, slab_rows, width), jnp.float32),
            pltpu.SemaphoreType.DMA((parts,)),
            pltpu.SemaphoreType.DMA((parts,)),
            pltpu.SemaphoreType.DMA((parts,)),
            pltpu.SemaphoreType.DMA((parts,)),
            pltpu.SemaphoreType.DMA((lanes,)),
            pltpu.SemaphoreType.DMA((lanes,)),
        ],
        compiler_params=pltpu.CompilerParams(
            collective_id=1, has_side_effects=True, vmem_limit_bytes=VMEM_BYTES
        ),
        cost_estimate=pl.CostEstimate(
            flops=2 * rows * lanes * slab_rows * width,
            bytes_accessed=20 * slab_rows * width * lanes,
            transcendentals=0,
        ),
    )(index, result)


def cut_kernel(starts, voxel_feats, slabs, held, arrived):
    part = lax.axis_index("mp")
    lanes, slab_rows, width = slabs.shape
    held_rows = held.shape[1]

    def copy(lane):
        first = pl.multiple_of(starts[1, lane], ALIGN)
        column = pl.multiple_of(part * width, width)
        return pltpu.make_async_copy(
            voxel_feats.at[pl.ds(first, held_rows), pl.ds(column, width)],
            held.at[lane],
            arrived.at[lane],
        )

    for lane in range(lanes):
        copy(lane).start()
    for lane in range(lanes):
        copy(lane).wait()
        rows = held[lane].astype(jnp.float32)
        ahead = starts[0, lane] - starts[1, lane]
        turned = pltpu.roll(rows, lax.rem(held_rows - ahead, held_rows), 0)
        slabs[lane] = turned[:slab_rows].astype(jnp.bfloat16)


def cut(starts, voxel_feats, slab_rows, parts):
    lanes = starts.shape[1]
    width = voxel_feats.shape[1] // parts
    return pl.pallas_call(
        cut_kernel,
        out_shape=jax.ShapeDtypeStruct((lanes, slab_rows, width), jnp.bfloat16),
        in_specs=[pl.BlockSpec(memory_space=pltpu.SMEM), pl.BlockSpec(memory_space=pl.ANY)],
        out_specs=pl.BlockSpec(memory_space=pltpu.VMEM),
        scratch_shapes=[
            pltpu.VMEM((lanes, slab_rows + ALIGN, width), jnp.bfloat16),
            pltpu.SemaphoreType.DMA((lanes,)),
        ],
        compiler_params=pltpu.CompilerParams(vmem_limit_bytes=VMEM_BYTES),
    )(starts, voxel_feats)


def place_kernel(starts, slabs, out, total):
    lanes, slab_rows, width = slabs.shape
    total[...] = jnp.zeros_like(total)
    for lane in range(lanes):
        rows = jnp.concatenate(
            [slabs[lane].astype(jnp.float32), jnp.zeros((ALIGN, width), jnp.float32)], axis=0
        )
        turned = pltpu.roll(rows, starts[0, lane] - starts[1, lane], 0)
        at = pl.ds(pl.multiple_of(starts[1, lane], ALIGN), slab_rows + ALIGN)
        total[at, :] += turned
    out[...] = total[...].astype(jnp.bfloat16)


def place(starts, slabs, capacity):
    width = slabs.shape[2]
    whole = pl.BlockSpec(memory_space=pltpu.VMEM)
    return pl.pallas_call(
        place_kernel,
        out_shape=jax.ShapeDtypeStruct((capacity, width), jnp.bfloat16),
        in_specs=[pl.BlockSpec(memory_space=pltpu.SMEM), whole],
        out_specs=whole,
        scratch_shapes=[pltpu.VMEM((capacity, width), jnp.float32)],
        compiler_params=pltpu.CompilerParams(vmem_limit_bytes=VMEM_BYTES),
    )(starts, slabs)


def layer_norm(values, gain):
    centred = values - jnp.mean(values, axis=-1, keepdims=True)
    spread = jnp.mean(centred * centred, axis=-1, keepdims=True)
    return (centred * lax.rsqrt(spread + EPSILON) * gain).astype(jnp.bfloat16)


def attention_kernel(
    head_dim,
    query_tile,
    query_from,
    patch_rows,
    gain,
    weights,
    attended,
    normed,
    queries,
    keys,
    values,
    held,
    mixed,
    arrived,
):
    groups, depth, triple = held.shape

    def copy(group):
        return pltpu.make_async_copy(
            weights.at[pl.ds(group * depth, depth)], held.at[group], arrived.at[group]
        )

    mixed[...] = jnp.zeros_like(mixed)
    for group in range(groups):
        copy(group).start()
    lanes = triple // 3
    group_heads = lanes // head_dim
    query_rows = attended.shape[0]
    normed[...] = layer_norm(patch_rows[...].astype(jnp.float32), gain[...])
    start = pl.multiple_of(query_from[0], query_rows)
    scale = head_dim ** (-0.5) * math.log2(math.e)
    lane_head = lax.broadcasted_iota(jnp.int32, (1, lanes), 1) // head_dim
    for group in range(groups):
        copy(group).wait()
        weight = held[group]
        queries[group] = (
            jnp.dot(
                normed[pl.ds(start, query_rows), :],
                weight[:, :lanes],
                preferred_element_type=jnp.float32,
            )
            * scale
        ).astype(jnp.bfloat16)
        both = jnp.dot(
            normed[...], weight[:, lanes:], preferred_element_type=jnp.float32
        ).astype(jnp.bfloat16)
        keys[group] = both[:, :lanes]
        values[group, :, :lanes] = both[:, lanes:]
        values[group, :, lanes:] = jnp.ones_like(both[:, lanes:])

    heads_once = 4
    chunks = query_rows // query_tile

    def some_heads(turn, carry):
        group = turn // (group_heads // heads_once)
        first_head = lax.rem(turn, group_heads // heads_once) * heads_once
        work = [(head, chunk) for head in range(heads_once) for chunk in range(chunks)]

        def rows_at(chunk):
            return slice(chunk * query_tile, (chunk + 1) * query_tile)

        def score(head, chunk):
            query = queries[group, rows_at(chunk), :]
            query = jnp.where(lane_head == first_head + head, query, jnp.zeros_like(query))
            return lax.dot_general(
                query,
                keys[group],
                (((1,), (1,)), ((), ())),
                preferred_element_type=jnp.float32,
            )

        def finish(head, chunk, exps):
            product = jnp.dot(exps, values[group], preferred_element_type=jnp.float32)
            result = product[:, :lanes] / product[:, lanes:]
            mine = lane_head == first_head + head
            at = rows_at(chunk)
            mixed[group, at, :] = jnp.where(mine, result, mixed[group, at, :])

        scores, exps = score(*work[0]), None
        for step, item in enumerate(work):
            later = score(*work[step + 1]) if step + 1 < len(work) else None
            highest = jnp.max(scores, axis=-1, keepdims=True)
            now = jnp.exp2((scores - highest).astype(jnp.bfloat16))
            if step:
                finish(*work[step - 1], exps)
            scores, exps = later, now
        finish(*work[-1], exps)
        return carry

    lax.fori_loop(0, groups * group_heads // heads_once, some_heads, 0)
    for group in range(groups):
        attended[:, group * lanes : (group + 1) * lanes] = mixed[group].astype(jnp.bfloat16)


def attention(patch_rows, gain, weights, query_from, query_rows, head_dim):
    rows, width = patch_rows.shape
    groups, triple = weights.shape[0] // width, weights.shape[1]
    lanes = triple // 3
    whole = pl.BlockSpec(memory_space=pltpu.VMEM)
    return pl.pallas_call(
        functools.partial(attention_kernel, head_dim, query_rows // 2),
        out_shape=jax.ShapeDtypeStruct((query_rows, groups * lanes), jnp.bfloat16),
        in_specs=[
            pl.BlockSpec(memory_space=pltpu.SMEM),
            whole,
            whole,
            pl.BlockSpec(memory_space=pl.ANY),
        ],
        out_specs=whole,
        scratch_shapes=[
            pltpu.VMEM((rows, width), jnp.bfloat16),
            pltpu.VMEM((groups, query_rows, lanes), jnp.bfloat16),
            pltpu.VMEM((groups, rows, lanes), jnp.bfloat16),
            pltpu.VMEM((groups, rows, 2 * lanes), jnp.bfloat16),
            pltpu.VMEM((groups, width, triple), jnp.bfloat16),
            pltpu.VMEM((groups, query_rows, lanes), jnp.float32),
            pltpu.SemaphoreType.DMA((groups,)),
        ],
        compiler_params=pltpu.CompilerParams(vmem_limit_bytes=VMEM_BYTES),
        cost_estimate=pl.CostEstimate(
            flops=4 * rows * query_rows * groups * lanes * 16,
            bytes_accessed=4 * rows * width,
            transcendentals=rows * query_rows * groups * 8,
        ),
    )(query_from, patch_rows, gain, weights)


def mlp_kernel(scalars, patch_rows, attended, gain, *refs):
    weights, result = refs[:-1], refs[-1]
    groups = len(weights)
    rows = attended.shape[0]
    depth = attended.shape[1] // groups
    hidden_part = (weights[0].shape[0] - depth) // 2
    proj_weight = [weights[group][:depth, :] for group in range(groups)]
    up_weight = [weights[group][depth : depth + hidden_part, :] for group in range(groups)]
    down_weight = [weights[group][depth + hidden_part :, :] for group in range(groups)]
    start = pl.multiple_of(scalars[0], rows)
    own = patch_rows[pl.ds(start, rows), :].astype(jnp.float32)
    mixed = None
    for group in range(groups):
        term = jnp.dot(
            attended[:, pl.ds(pl.multiple_of(scalars[1 + group] * depth, depth), depth)],
            proj_weight[group],
            preferred_element_type=jnp.float32,
        ).astype(jnp.bfloat16).astype(jnp.float32)
        mixed = term if mixed is None else mixed + term
    hidden = (own + mixed).astype(jnp.bfloat16).astype(jnp.float32)
    normed = layer_norm(hidden, gain[...])
    total = None
    for group in range(groups):
        expanded = jnp.dot(normed, up_weight[group], preferred_element_type=jnp.float32)
        expanded = (
            0.5 * expanded * (1.0 + lax.erf(expanded * math.sqrt(0.5)))
        ).astype(jnp.bfloat16)
        term = jnp.dot(
            expanded, down_weight[group], preferred_element_type=jnp.float32
        ).astype(jnp.bfloat16).astype(jnp.float32)
        total = term if total is None else total + term
    final = (hidden + total).astype(jnp.bfloat16)
    width = result.shape[2]
    for part in range(result.shape[0]):
        result[part] = final[:, part * width : (part + 1) * width]


def mlp(patch_rows, attended, gain, weights, scalars):
    whole = pl.BlockSpec(memory_space=pltpu.VMEM)
    rows, width = attended.shape
    groups, hidden = len(weights), weights[0].shape[1]
    return pl.pallas_call(
        mlp_kernel,
        out_shape=jax.ShapeDtypeStruct((groups, rows, width // groups), jnp.bfloat16),
        in_specs=[pl.BlockSpec(memory_space=pltpu.SMEM)] + [whole] * (3 + groups),
        out_specs=whole,
        compiler_params=pltpu.CompilerParams(vmem_limit_bytes=VMEM_BYTES),
        cost_estimate=pl.CostEstimate(
            flops=4 * rows * width * hidden * groups,
            bytes_accessed=8 * width * hidden * groups,
            transcendentals=rows * hidden * groups,
        ),
    )(scalars, patch_rows, attended, gain, *weights)


def per_device(
    voxel_feats,
    slot_rank,
    curve_order,
    patch_shift,
    qkv_weight,
    proj_weight,
    up_weight,
    down_weight,
    norm_gains,
):
    bricks = lax.axis_size("brick")
    model_parts = lax.axis_size("mp")
    my_index = lax.axis_index("brick")
    part_index = lax.axis_index("mp")
    capacity = voxel_feats.shape[0]
    shard_rows = curve_order.shape[0]
    pair_rows = 3 * (shard_rows // 8)
    width_full = voxel_feats.shape[1]
    width_part = width_full // model_parts
    quarter_rows = shard_rows // model_parts
    head_dim = width_full // HEADS
    offset = patch_shift[0].astype(jnp.uint32)
    latest = capacity - pair_rows

    triple = qkv_weight.shape[1]
    spot = jnp.arange(triple, dtype=jnp.int32)
    kind, within = spot // width_part, spot % width_part
    origin = (within // head_dim) * 3 * head_dim + kind * head_dim + within % head_dim
    shuffle = (spot[:, None] == origin[None, :]).astype(jnp.bfloat16)
    qkv_sorted = jnp.dot(
        qkv_weight, shuffle, preferred_element_type=jnp.float32
    ).astype(jnp.bfloat16)
    qkv_all = lax.all_gather(qkv_sorted, "mp", axis=0, tiled=True)
    patches = shard_rows // PATCH
    half = model_parts // patches
    held = jnp.concatenate([proj_weight, up_weight, down_weight], axis=0)
    far = [held] + [passed(held, patches, step, 0) for step in range(1, patches)]

    lane_ids = jnp.arange(4, dtype=jnp.int32)
    lane_targets = wrapped(my_index - (lane_ids - 1), bricks)
    low = lane_targets * shard_rows
    below = slot_rank[:, None] < low[None, :]
    run_starts = jnp.sum(below.astype(jnp.int32), axis=0)
    slab_starts = jnp.minimum(run_starts, latest)
    aligned = jnp.minimum(slab_starts // ALIGN * ALIGN, latest - ALIGN)
    starts = jnp.stack([slab_starts, aligned])

    source_brick = curve_order // capacity
    source_slot = curve_order - source_brick * capacity
    source_lane = wrapped(source_brick - my_index + 1, bricks)
    from_lane = source_lane[:, None] == lane_ids[None, :]
    first_slot = jnp.min(jnp.where(from_lane, source_slot[:, None], latest), axis=0)
    first_of_row = jnp.sum(jnp.where(from_lane, first_slot[None, :], 0), axis=1)
    recv_index = source_lane * pair_rows + source_slot - first_of_row
    empty = jnp.full((PATCH,), -1, jnp.int32)
    index = lax.dynamic_slice_in_dim(
        jnp.concatenate([empty, recv_index, empty]), offset, shard_rows + PATCH, 0
    )

    slabs = cut(starts, voxel_feats, pair_rows, model_parts)
    patch_rows = enter(index[None, :], slabs, bricks, model_parts)
    *far, patch_rows = lax.optimization_barrier((*far, patch_rows))
    weights, origins = [], []
    for near_step in range(half):
        for patch_step in range(patches):
            value = far[patch_step]
            weights.append(passed(value, patches, 0, near_step) if near_step else value)
            patch = lax.rem(part_index // half + patches - patch_step, patches)
            place_in = lax.rem(part_index + half - near_step, half)
            origins.append(patch * half + place_in)
    query_from = (lax.rem(part_index * quarter_rows, PATCH))[None]
    attended = attention(
        patch_rows, norm_gains[0:1], qkv_all, query_from, quarter_rows, head_dim
    )
    scalars = jnp.concatenate([query_from, jnp.stack(origins)])
    result = mlp(patch_rows, attended, norm_gains[1:2], weights, scalars)
    returned = leave(index[None, :], result, bricks, 4, pair_rows)
    return place(starts, returned, capacity)


def solution(mesh):
    return jax.shard_map(
        per_device,
        mesh=mesh,
        in_specs=(
            P("brick", None),
            P("brick"),
            P("brick"),
            P(),
            P(None, "mp"),
            P("mp", None),
            P(None, "mp"),
            P("mp", None),
            P(),
        ),
        out_specs=P("brick", "mp"),
        check_vma=False,
    )
```

```python
import functools
import math

import jax
import jax.numpy as jnp
from jax import lax
from jax.experimental import pallas as pl
from jax.experimental.pallas import tpu as pltpu
from jax.sharding import PartitionSpec as P

HEADS = 32
PATCH = 1024
EPSILON = 1e-05
ALIGN = 16
VMEM_BYTES = 56 * 1024 * 1024


MESH = pl.DeviceIdType.MESH


def passed(value, patches, patch_step, near_step):
    parts = lax.axis_size("mp")
    half = parts // patches
    pairs = []
    for source in range(parts):
        patch, place = source // half, source % half
        target = (patch + patch_step) % patches * half + (place + near_step) % half
        pairs.append((source, target))
    return lax.ppermute(value, "mp", pairs)


def wrapped(value, count):
    value = jnp.where(value < 0, value + count, value)
    return jnp.where(value >= count, value - count, value)


def greet_all(bricks, parts, wide):
    brick, part = lax.axis_index("brick"), lax.axis_index("mp")
    barrier = pltpu.get_barrier_semaphore()
    peers = [(0, step) for step in range(1, parts)]
    peers += [(away, step) for away in (-1, 1) for step in range(parts if wide else 1)]
    peers += [(-2, 0), (2, 0)]
    for away, step in peers:
        pl.semaphore_signal(
            barrier,
            inc=1,
            device_id=(lax.rem(brick + away + bricks, bricks), lax.rem(part + step, parts)),
            device_id_type=MESH,
        )
    pl.semaphore_wait(barrier, len(peers))


def enter_kernel(
    bricks,
    parts,
    index,
    slabs,
    patch_rows,
    arrived,
    total,
    merged,
    window_in,
    head_in,
    column_index,
    lane_send,
    lane_recv,
    far_send,
    far_recv,
    near_send,
    near_recv,
    head_send,
    head_recv,
):
    brick, part = lax.axis_index("brick"), lax.axis_index("mp")
    slab_rows, width = slabs.shape[1], slabs.shape[2]
    rows = index.shape[1]
    tile = 1024
    lane_width = column_index.shape[1]
    greet_all(bricks, parts, False)

    def lane_copy(lane):
        return pltpu.make_async_remote_copy(
            src_ref=slabs.at[lane],
            dst_ref=arrived.at[lane],
            send_sem=lane_send.at[lane],
            recv_sem=lane_recv.at[lane],
            device_id=(lax.rem(brick - lane + 1 + bricks, bricks), part),
            device_id_type=MESH,
        )

    for lane in (3, 0, 2):
        lane_copy(lane).start()
    for start in range(0, rows, tile):
        column_index[start : start + tile, :] = jnp.broadcast_to(
            index[:, start : start + tile], (lane_width, tile)
        ).T.astype(jnp.int16)

    def merge(lane, source, first):
        def one_tile(step, carry):
            at = pl.ds(pl.multiple_of(step * tile, tile), tile)
            mine = column_index[at, :]
            spots = lax.broadcasted_iota(jnp.int32, (tile, lane_width), 1) + lane * slab_rows
            one, zero = jnp.ones((), jnp.bfloat16), jnp.zeros((), jnp.bfloat16)
            chosen = jnp.concatenate(
                [
                    jnp.where(mine == (spots + start).astype(jnp.int16), one, zero)
                    for start in range(0, slab_rows, lane_width)
                ],
                axis=1,
            )
            term = jnp.dot(chosen, source, preferred_element_type=jnp.float32)
            if first:
                total[at, :] = term
            else:
                total[at, :] += term
            return carry

        lax.fori_loop(0, rows // tile, one_tile, 0)

    merge(1, slabs[1], True)
    for lane in (2, 0, 3):
        lane_copy(lane).wait()
        merge(lane, arrived[lane], False)
    merged[...] = total[...].astype(jnp.bfloat16)

    patches = (rows - PATCH) // PATCH
    half = parts // patches
    patch, place = part // half, lax.rem(part, half)
    last = patches - 1

    def rows_of(which):
        return pl.ds(pl.multiple_of((which + 1) * PATCH, PATCH), PATCH)

    head_copy = pltpu.make_async_remote_copy(
        src_ref=merged.at[pl.ds(0, PATCH)],
        dst_ref=head_in,
        send_sem=head_send.at[0],
        recv_sem=head_recv.at[0],
        device_id=(lax.rem(brick - 1 + bricks, bricks), part),
        device_id_type=MESH,
    )
    head_copy.start()

    def far_target(step):
        return lax.rem(patch + step, patches)

    def far_copy(step):
        return pltpu.make_async_remote_copy(
            src_ref=merged.at[rows_of(far_target(step))],
            dst_ref=window_in.at[part],
            send_sem=far_send.at[step],
            recv_sem=far_recv.at[step],
            device_id=(brick, far_target(step) * half + place),
            device_id_type=MESH,
        )

    def near_copy(step, far_step):
        source = lax.rem(patch - far_step + patches, patches) * half + place
        return pltpu.make_async_remote_copy(
            src_ref=window_in.at[source],
            dst_ref=window_in.at[source],
            send_sem=near_send.at[step, far_step],
            recv_sem=near_recv.at[step, far_step],
            device_id=(brick, patch * half + lax.rem(place + step, half)),
            device_id_type=MESH,
        )

    def start_far(late):
        for step in range(1, patches):

            @pl.when((far_target(step) == last) if late else (far_target(step) != last))
            def _():
                far_copy(step).start()

    def start_own():
        window_in[part] = merged[rows_of(patch), :]
        for step in range(1, half):
            near_copy(step, 0).start()

    start_far(False)

    @pl.when(patch != last)
    def _():
        start_own()

    head_copy.wait_recv()
    merged[rows - PATCH :, :] += head_in[...]
    start_far(True)

    @pl.when(patch == last)
    def _():
        start_own()

    for far_step in range(1, patches):
        far_copy(far_step).wait()
        for step in range(1, half):
            near_copy(step, far_step).start()
    for far_step in range(patches):
        for step in range(1, half):
            near_copy(step, far_step).wait()
    head_copy.wait_send()
    for source in range(parts):
        patch_rows[:, source * width : (source + 1) * width] = window_in[source]


def enter(index, slabs, bricks, parts):
    lanes, slab_rows, width = slabs.shape
    rows = index.shape[1]
    whole = pl.BlockSpec(memory_space=pltpu.VMEM)
    return pl.pallas_call(
        functools.partial(enter_kernel, bricks, parts),
        out_shape=jax.ShapeDtypeStruct((PATCH, width * parts), jnp.bfloat16),
        in_specs=[whole, whole],
        out_specs=whole,
        scratch_shapes=[
            pltpu.VMEM((lanes, slab_rows, width), jnp.bfloat16),
            pltpu.VMEM((rows, width), jnp.float32),
            pltpu.VMEM((rows, width), jnp.bfloat16),
            pltpu.VMEM((parts, PATCH, width), jnp.bfloat16),
            pltpu.VMEM((PATCH, width), jnp.bfloat16),
            pltpu.VMEM((rows, 128), jnp.int16),
            pltpu.SemaphoreType.DMA((lanes,)),
            pltpu.SemaphoreType.DMA((lanes,)),
            pltpu.SemaphoreType.DMA((parts,)),
            pltpu.SemaphoreType.DMA((parts,)),
            pltpu.SemaphoreType.DMA((parts, parts)),
            pltpu.SemaphoreType.DMA((parts, parts)),
            pltpu.SemaphoreType.DMA((1,)),
            pltpu.SemaphoreType.DMA((1,)),
        ],
        compiler_params=pltpu.CompilerParams(
            collective_id=0, has_side_effects=True, vmem_limit_bytes=VMEM_BYTES
        ),
        cost_estimate=pl.CostEstimate(
            flops=2 * rows * lanes * slab_rows * width,
            bytes_accessed=20 * slab_rows * width * lanes,
            transcendentals=0,
        ),
    )(index, slabs)


def leave_kernel(
    bricks,
    parts,
    index,
    result,
    arrived,
    rows_in,
    leaving,
    total,
    window_send,
    window_recv,
    tail_send,
    tail_recv,
    lane_send,
    lane_recv,
):
    brick, part = lax.axis_index("brick"), lax.axis_index("mp")
    lanes, slab_rows, width = leaving.shape
    quarter = result.shape[1]
    rows = rows_in.shape[0]
    last = rows - PATCH
    greet_all(bricks, parts, True)

    def row_start(source):
        return PATCH + source * quarter

    def tail_copy(step):
        target = lax.rem(part + step, parts)
        start = pl.multiple_of(jnp.maximum(row_start(part) - last, 0), quarter)
        return pltpu.make_async_remote_copy(
            src_ref=result.at[target],
            dst_ref=rows_in.at[pl.ds(start, quarter)],
            send_sem=tail_send.at[step],
            recv_sem=tail_recv.at[part],
            device_id=(lax.rem(brick + 1, bricks), target),
            device_id_type=MESH,
        )

    def window_copy(step):
        target = lax.rem(part + step, parts)
        start = pl.multiple_of(row_start(part), quarter)
        return pltpu.make_async_remote_copy(
            src_ref=result.at[target],
            dst_ref=rows_in.at[pl.ds(start, quarter)],
            send_sem=window_send.at[step],
            recv_sem=window_recv.at[step],
            device_id=(brick, target),
            device_id_type=MESH,
        )

    def tail_arrival(source):
        return pltpu.make_async_remote_copy(
            src_ref=result.at[0],
            dst_ref=rows_in.at[pl.ds(row_start(source) - last, quarter)],
            send_sem=tail_send.at[0],
            recv_sem=tail_recv.at[source],
            device_id=(lax.rem(brick + 1, bricks), part),
            device_id_type=MESH,
        )

    def window_arrival(step):
        source = lax.rem(part - step + parts, parts)
        return pltpu.make_async_remote_copy(
            src_ref=result.at[0],
            dst_ref=rows_in.at[pl.ds(pl.multiple_of(row_start(source), quarter), quarter)],
            send_sem=window_send.at[step],
            recv_sem=window_recv.at[step],
            device_id=(brick, source),
            device_id_type=MESH,
        )

    sends_tail = row_start(part) >= last

    @pl.when(sends_tail)
    def _():
        for step in range(parts):
            tail_copy(step).start()

    for step in range(1, parts):
        window_copy(step).start()
    rows_in[pl.ds(pl.multiple_of(row_start(part), quarter), quarter), :] = result[part]
    for step in range(1, parts):
        window_arrival(step).wait_recv()
    def lane_copy(lane):
        return pltpu.make_async_remote_copy(
            src_ref=leaving.at[lane],
            dst_ref=arrived.at[lane],
            send_sem=lane_send.at[lane],
            recv_sem=lane_recv.at[lane],
            device_id=(lax.rem(brick + lane - 1 + bricks, bricks), part),
            device_id_type=MESH,
        )

    def spread(lane, start, stop):
        spots = lax.broadcasted_iota(jnp.int32, (slab_rows, stop - start), 0)
        mine = (index[:, start:stop] - lane * slab_rows).astype(jnp.int16)
        one, zero = jnp.ones((), jnp.bfloat16), jnp.zeros((), jnp.bfloat16)
        chosen = jnp.where(mine == spots.astype(jnp.int16), one, zero)
        return jnp.dot(chosen, rows_in[start:stop, :], preferred_element_type=jnp.float32)

    for lane in (3, 0, 2):
        total[lane] = spread(lane, PATCH, rows)
    for source in range(parts):
        if row_start(source) >= last:
            tail_arrival(source).wait_recv()
    for lane in (3, 0, 2):
        leaving[lane] = (total[lane] + spread(lane, 0, PATCH)).astype(jnp.bfloat16)
        lane_copy(lane).start()
    arrived[1] = spread(1, 0, rows).astype(jnp.bfloat16)
    for lane in (2, 0, 3):
        lane_copy(lane).wait()

    for step in range(1, parts):
        window_copy(step).wait_send()

    @pl.when(sends_tail)
    def _():
        for step in range(parts):
            tail_copy(step).wait_send()


def leave(index, result, bricks, lanes, slab_rows):
    parts, quarter, width = result.shape
    rows = index.shape[1]
    whole = pl.BlockSpec(memory_space=pltpu.VMEM)
    return pl.pallas_call(
        functools.partial(leave_kernel, bricks, parts),
        out_shape=jax.ShapeDtypeStruct((lanes, slab_rows, width), jnp.bfloat16),
        in_specs=[whole, whole],
        out_specs=whole,
        scratch_shapes=[
            pltpu.VMEM((rows, width), jnp.bfloat16),
            pltpu.VMEM((lanes, slab_rows, width), jnp.bfloat16),
            pltpu.VMEM((lanes, slab_rows, width), jnp.float32),
            pltpu.SemaphoreType.DMA((parts,)),
            pltpu.SemaphoreType.DMA((parts,)),
            pltpu.SemaphoreType.DMA((parts,)),
            pltpu.SemaphoreType.DMA((parts,)),
            pltpu.SemaphoreType.DMA((lanes,)),
            pltpu.SemaphoreType.DMA((lanes,)),
        ],
        compiler_params=pltpu.CompilerParams(
            collective_id=1, has_side_effects=True, vmem_limit_bytes=VMEM_BYTES
        ),
        cost_estimate=pl.CostEstimate(
            flops=2 * rows * lanes * slab_rows * width,
            bytes_accessed=20 * slab_rows * width * lanes,
            transcendentals=0,
        ),
    )(index, result)


def cut_kernel(starts, voxel_feats, slabs, held, arrived):
    part = lax.axis_index("mp")
    lanes, slab_rows, width = slabs.shape
    held_rows = held.shape[1]

    def copy(lane):
        first = pl.multiple_of(starts[1, lane], ALIGN)
        column = pl.multiple_of(part * width, width)
        return pltpu.make_async_copy(
            voxel_feats.at[pl.ds(first, held_rows), pl.ds(column, width)],
            held.at[lane],
            arrived.at[lane],
        )

    for lane in range(lanes):
        copy(lane).start()
    for lane in range(lanes):
        copy(lane).wait()
        rows = held[lane].astype(jnp.float32)
        ahead = starts[0, lane] - starts[1, lane]
        turned = pltpu.roll(rows, lax.rem(held_rows - ahead, held_rows), 0)
        slabs[lane] = turned[:slab_rows].astype(jnp.bfloat16)


def cut(starts, voxel_feats, slab_rows, parts):
    lanes = starts.shape[1]
    width = voxel_feats.shape[1] // parts
    return pl.pallas_call(
        cut_kernel,
        out_shape=jax.ShapeDtypeStruct((lanes, slab_rows, width), jnp.bfloat16),
        in_specs=[pl.BlockSpec(memory_space=pltpu.SMEM), pl.BlockSpec(memory_space=pl.ANY)],
        out_specs=pl.BlockSpec(memory_space=pltpu.VMEM),
        scratch_shapes=[
            pltpu.VMEM((lanes, slab_rows + ALIGN, width), jnp.bfloat16),
            pltpu.SemaphoreType.DMA((lanes,)),
        ],
        compiler_params=pltpu.CompilerParams(vmem_limit_bytes=VMEM_BYTES),
    )(starts, voxel_feats)


def place_kernel(starts, slabs, out, total):
    lanes, slab_rows, width = slabs.shape
    total[...] = jnp.zeros_like(total)
    for lane in range(lanes):
        rows = jnp.concatenate(
            [slabs[lane].astype(jnp.float32), jnp.zeros((ALIGN, width), jnp.float32)], axis=0
        )
        turned = pltpu.roll(rows, starts[0, lane] - starts[1, lane], 0)
        at = pl.ds(pl.multiple_of(starts[1, lane], ALIGN), slab_rows + ALIGN)
        total[at, :] += turned
    out[...] = total[...].astype(jnp.bfloat16)


def place(starts, slabs, capacity):
    width = slabs.shape[2]
    whole = pl.BlockSpec(memory_space=pltpu.VMEM)
    return pl.pallas_call(
        place_kernel,
        out_shape=jax.ShapeDtypeStruct((capacity, width), jnp.bfloat16),
        in_specs=[pl.BlockSpec(memory_space=pltpu.SMEM), whole],
        out_specs=whole,
        scratch_shapes=[pltpu.VMEM((capacity, width), jnp.float32)],
        compiler_params=pltpu.CompilerParams(vmem_limit_bytes=VMEM_BYTES),
    )(starts, slabs)


def layer_norm(values, gain):
    centred = values - jnp.mean(values, axis=-1, keepdims=True)
    spread = jnp.mean(centred * centred, axis=-1, keepdims=True)
    return (centred * lax.rsqrt(spread + EPSILON) * gain).astype(jnp.bfloat16)


def attention_kernel(
    head_dim,
    query_tile,
    query_from,
    patch_rows,
    gain,
    weights,
    attended,
    normed,
    queries,
    keys,
    values,
    held,
    mixed,
    arrived,
):
    groups, depth, triple = held.shape

    def copy(group):
        return pltpu.make_async_copy(
            weights.at[pl.ds(group * depth, depth)], held.at[group], arrived.at[group]
        )

    mixed[...] = jnp.zeros_like(mixed)
    for group in range(groups):
        copy(group).start()
    lanes = triple // 3
    group_heads = lanes // head_dim
    query_rows = attended.shape[0]
    normed[...] = layer_norm(patch_rows[...].astype(jnp.float32), gain[...])
    start = pl.multiple_of(query_from[0], query_rows)
    scale = head_dim ** (-0.5) * math.log2(math.e)
    lane_head = lax.broadcasted_iota(jnp.int32, (1, lanes), 1) // head_dim
    for group in range(groups):
        copy(group).wait()
        weight = held[group]
        queries[group] = (
            jnp.dot(
                normed[pl.ds(start, query_rows), :],
                weight[:, :lanes],
                preferred_element_type=jnp.float32,
            )
            * scale
        ).astype(jnp.bfloat16)
        both = jnp.dot(
            normed[...], weight[:, lanes:], preferred_element_type=jnp.float32
        ).astype(jnp.bfloat16)
        keys[group] = both[:, :lanes]
        values[group, :, :lanes] = both[:, lanes:]
        values[group, :, lanes:] = jnp.ones_like(both[:, lanes:])

    heads_once = group_heads
    chunks = query_rows // query_tile

    def some_heads(turn, carry):
        group = turn // (group_heads // heads_once)
        first_head = lax.rem(turn, group_heads // heads_once) * heads_once
        work = [(head, chunk) for head in range(heads_once) for chunk in range(chunks)]

        def rows_at(chunk):
            return slice(chunk * query_tile, (chunk + 1) * query_tile)

        def score(head, chunk):
            query = queries[group, rows_at(chunk), :]
            query = jnp.where(lane_head == first_head + head, query, jnp.zeros_like(query))
            return lax.dot_general(
                query,
                keys[group],
                (((1,), (1,)), ((), ())),
                preferred_element_type=jnp.float32,
            )

        def finish(head, chunk, exps):
            product = jnp.dot(exps, values[group], preferred_element_type=jnp.float32)
            result = product[:, :lanes] / product[:, lanes:]
            mine = lane_head == first_head + head
            at = rows_at(chunk)
            mixed[group, at, :] = jnp.where(mine, result, mixed[group, at, :])

        scores, exps = score(*work[0]), None
        for step, item in enumerate(work):
            later = score(*work[step + 1]) if step + 1 < len(work) else None
            highest = jnp.max(scores, axis=-1, keepdims=True)
            now = jnp.exp2((scores - highest).astype(jnp.bfloat16))
            if step:
                finish(*work[step - 1], exps)
            scores, exps = later, now
        finish(*work[-1], exps)
        return carry

    lax.fori_loop(0, groups * group_heads // heads_once, some_heads, 0)
    for group in range(groups):
        attended[:, group * lanes : (group + 1) * lanes] = mixed[group].astype(jnp.bfloat16)


def attention(patch_rows, gain, weights, query_from, query_rows, head_dim):
    rows, width = patch_rows.shape
    groups, triple = weights.shape[0] // width, weights.shape[1]
    lanes = triple // 3
    whole = pl.BlockSpec(memory_space=pltpu.VMEM)
    return pl.pallas_call(
        functools.partial(attention_kernel, head_dim, query_rows // 2),
        out_shape=jax.ShapeDtypeStruct((query_rows, groups * lanes), jnp.bfloat16),
        in_specs=[
            pl.BlockSpec(memory_space=pltpu.SMEM),
            whole,
            whole,
            pl.BlockSpec(memory_space=pl.ANY),
        ],
        out_specs=whole,
        scratch_shapes=[
            pltpu.VMEM((rows, width), jnp.bfloat16),
            pltpu.VMEM((groups, query_rows, lanes), jnp.bfloat16),
            pltpu.VMEM((groups, rows, lanes), jnp.bfloat16),
            pltpu.VMEM((groups, rows, 2 * lanes), jnp.bfloat16),
            pltpu.VMEM((groups, width, triple), jnp.bfloat16),
            pltpu.VMEM((groups, query_rows, lanes), jnp.float32),
            pltpu.SemaphoreType.DMA((groups,)),
        ],
        compiler_params=pltpu.CompilerParams(vmem_limit_bytes=VMEM_BYTES),
        cost_estimate=pl.CostEstimate(
            flops=4 * rows * query_rows * groups * lanes * 16,
            bytes_accessed=4 * rows * width,
            transcendentals=rows * query_rows * groups * 8,
        ),
    )(query_from, patch_rows, gain, weights)


def mlp_kernel(scalars, patch_rows, attended, gain, *refs):
    weights, result = refs[:-1], refs[-1]
    groups = len(weights)
    rows = attended.shape[0]
    depth = attended.shape[1] // groups
    hidden_part = (weights[0].shape[0] - depth) // 2
    proj_weight = [weights[group][:depth, :] for group in range(groups)]
    up_weight = [weights[group][depth : depth + hidden_part, :] for group in range(groups)]
    down_weight = [weights[group][depth + hidden_part :, :] for group in range(groups)]
    start = pl.multiple_of(scalars[0], rows)
    own = patch_rows[pl.ds(start, rows), :].astype(jnp.float32)
    mixed = None
    for group in range(groups):
        term = jnp.dot(
            attended[:, pl.ds(pl.multiple_of(scalars[1 + group] * depth, depth), depth)],
            proj_weight[group],
            preferred_element_type=jnp.float32,
        ).astype(jnp.bfloat16).astype(jnp.float32)
        mixed = term if mixed is None else mixed + term
    hidden = (own + mixed).astype(jnp.bfloat16).astype(jnp.float32)
    normed = layer_norm(hidden, gain[...])

    def widen(group):
        return jnp.dot(normed, up_weight[group], preferred_element_type=jnp.float32)

    total, expanded = None, widen(0)
    for group in range(groups):
        later = widen(group + 1) if group + 1 < groups else None
        expanded = (
            0.5 * expanded * (1.0 + lax.erf(expanded * math.sqrt(0.5)))
        ).astype(jnp.bfloat16)
        term = jnp.dot(
            expanded, down_weight[group], preferred_element_type=jnp.float32
        ).astype(jnp.bfloat16).astype(jnp.float32)
        total = term if total is None else total + term
        expanded = later
    final = (hidden + total).astype(jnp.bfloat16)
    width = result.shape[2]
    for part in range(result.shape[0]):
        result[part] = final[:, part * width : (part + 1) * width]


def mlp(patch_rows, attended, gain, weights, scalars):
    whole = pl.BlockSpec(memory_space=pltpu.VMEM)
    rows, width = attended.shape
    groups, hidden = len(weights), weights[0].shape[1]
    return pl.pallas_call(
        mlp_kernel,
        out_shape=jax.ShapeDtypeStruct((groups, rows, width // groups), jnp.bfloat16),
        in_specs=[pl.BlockSpec(memory_space=pltpu.SMEM)] + [whole] * (3 + groups),
        out_specs=whole,
        compiler_params=pltpu.CompilerParams(vmem_limit_bytes=VMEM_BYTES),
        cost_estimate=pl.CostEstimate(
            flops=4 * rows * width * hidden * groups,
            bytes_accessed=8 * width * hidden * groups,
            transcendentals=rows * hidden * groups,
        ),
    )(scalars, patch_rows, attended, gain, *weights)


def per_device(
    voxel_feats,
    slot_rank,
    curve_order,
    patch_shift,
    qkv_weight,
    proj_weight,
    up_weight,
    down_weight,
    norm_gains,
):
    bricks = lax.axis_size("brick")
    model_parts = lax.axis_size("mp")
    my_index = lax.axis_index("brick")
    part_index = lax.axis_index("mp")
    capacity = voxel_feats.shape[0]
    shard_rows = curve_order.shape[0]
    pair_rows = 3 * (shard_rows // 8)
    width_full = voxel_feats.shape[1]
    width_part = width_full // model_parts
    quarter_rows = shard_rows // model_parts
    head_dim = width_full // HEADS
    offset = patch_shift[0].astype(jnp.uint32)
    latest = capacity - pair_rows

    triple = qkv_weight.shape[1]
    spot = jnp.arange(triple, dtype=jnp.int32)
    kind, within = spot // width_part, spot % width_part
    origin = (within // head_dim) * 3 * head_dim + kind * head_dim + within % head_dim
    shuffle = (spot[:, None] == origin[None, :]).astype(jnp.bfloat16)
    qkv_sorted = jnp.dot(
        qkv_weight, shuffle, preferred_element_type=jnp.float32
    ).astype(jnp.bfloat16)
    qkv_all = lax.all_gather(qkv_sorted, "mp", axis=0, tiled=True)
    patches = shard_rows // PATCH
    half = model_parts // patches
    held = jnp.concatenate([proj_weight, up_weight, down_weight], axis=0)
    far = [held] + [passed(held, patches, step, 0) for step in range(1, patches)]

    lane_ids = jnp.arange(4, dtype=jnp.int32)
    lane_targets = wrapped(my_index - (lane_ids - 1), bricks)
    low = lane_targets * shard_rows
    below = slot_rank[:, None] < low[None, :]
    run_starts = jnp.sum(below.astype(jnp.int32), axis=0)
    slab_starts = jnp.minimum(run_starts, latest)
    aligned = jnp.minimum(slab_starts // ALIGN * ALIGN, latest - ALIGN)
    starts = jnp.stack([slab_starts, aligned])

    source_brick = curve_order // capacity
    source_slot = curve_order - source_brick * capacity
    source_lane = wrapped(source_brick - my_index + 1, bricks)
    from_lane = source_lane[:, None] == lane_ids[None, :]
    first_slot = jnp.min(jnp.where(from_lane, source_slot[:, None], latest), axis=0)
    first_of_row = jnp.sum(jnp.where(from_lane, first_slot[None, :], 0), axis=1)
    recv_index = source_lane * pair_rows + source_slot - first_of_row
    empty = jnp.full((PATCH,), -1, jnp.int32)
    index = lax.dynamic_slice_in_dim(
        jnp.concatenate([empty, recv_index, empty]), offset, shard_rows + PATCH, 0
    )

    slabs = cut(starts, voxel_feats, pair_rows, model_parts)
    patch_rows = enter(index[None, :], slabs, bricks, model_parts)
    *far, patch_rows = lax.optimization_barrier((*far, patch_rows))
    weights, origins = [], []
    for near_step in range(half):
        for patch_step in range(patches):
            value = far[patch_step]
            weights.append(passed(value, patches, 0, near_step) if near_step else value)
            patch = lax.rem(part_index // half + patches - patch_step, patches)
            place_in = lax.rem(part_index + half - near_step, half)
            origins.append(patch * half + place_in)
    query_from = (lax.rem(part_index * quarter_rows, PATCH))[None]
    attended = attention(
        patch_rows, norm_gains[0:1], qkv_all, query_from, quarter_rows, head_dim
    )
    scalars = jnp.concatenate([query_from, jnp.stack(origins)])
    result = mlp(patch_rows, attended, norm_gains[1:2], weights, scalars)
    returned = leave(index[None, :], result, bricks, 4, pair_rows)
    return place(starts, returned, capacity)


def solution(mesh):
    return jax.shard_map(
        per_device,
        mesh=mesh,
        in_specs=(
            P("brick", None),
            P("brick"),
            P("brick"),
            P(),
            P(None, "mp"),
            P("mp", None),
            P(None, "mp"),
            P("mp", None),
            P(),
        ),
        out_specs=P("brick", "mp"),
        check_vma=False,
    )
```

```python
import functools
import math

import jax
import jax.numpy as jnp
from jax import lax
from jax.experimental import pallas as pl
from jax.experimental.pallas import tpu as pltpu
from jax.sharding import PartitionSpec as P

HEADS = 32
PATCH = 1024
EPSILON = 1e-05
ALIGN = 16
VMEM_BYTES = 56 * 1024 * 1024


MESH = pl.DeviceIdType.MESH


def passed(value, patches, patch_step, near_step):
    parts = lax.axis_size("mp")
    half = parts // patches
    pairs = []
    for source in range(parts):
        patch, place = source // half, source % half
        target = (patch + patch_step) % patches * half + (place + near_step) % half
        pairs.append((source, target))
    return lax.ppermute(value, "mp", pairs)


def wrapped(value, count):
    value = jnp.where(value < 0, value + count, value)
    return jnp.where(value >= count, value - count, value)


def greet_all(bricks, parts):
    brick, part = lax.axis_index("brick"), lax.axis_index("mp")
    barrier = pltpu.get_barrier_semaphore()
    peers = [(0, step) for step in range(1, parts)]
    peers += [(away, 0) for away in (-2, -1, 1, 2)]
    for away, step in peers:
        pl.semaphore_signal(
            barrier,
            inc=1,
            device_id=(lax.rem(brick + away + bricks, bricks), lax.rem(part + step, parts)),
            device_id_type=MESH,
        )
    pl.semaphore_wait(barrier, len(peers))


def enter_kernel(
    bricks,
    parts,
    index,
    slabs,
    patch_rows,
    arrived,
    total,
    merged,
    window_in,
    head_in,
    column_index,
    lane_send,
    lane_recv,
    far_send,
    far_recv,
    near_send,
    near_recv,
    head_send,
    head_recv,
):
    brick, part = lax.axis_index("brick"), lax.axis_index("mp")
    slab_rows, width = slabs.shape[1], slabs.shape[2]
    rows = index.shape[1]
    tile = 1024
    lane_width = column_index.shape[1]
    greet_all(bricks, parts)

    def lane_copy(lane):
        return pltpu.make_async_remote_copy(
            src_ref=slabs.at[lane],
            dst_ref=arrived.at[lane],
            send_sem=lane_send.at[lane],
            recv_sem=lane_recv.at[lane],
            device_id=(lax.rem(brick - lane + 1 + bricks, bricks), part),
            device_id_type=MESH,
        )

    for lane in (3, 0, 2):
        lane_copy(lane).start()
    for start in range(0, rows, tile):
        column_index[start : start + tile, :] = jnp.broadcast_to(
            index[:, start : start + tile], (lane_width, tile)
        ).T.astype(jnp.int16)

    def merge(lane, source, first):
        def one_tile(step, carry):
            at = pl.ds(pl.multiple_of(step * tile, tile), tile)
            mine = column_index[at, :]
            spots = lax.broadcasted_iota(jnp.int32, (tile, lane_width), 1) + lane * slab_rows
            one, zero = jnp.ones((), jnp.bfloat16), jnp.zeros((), jnp.bfloat16)
            chosen = jnp.concatenate(
                [
                    jnp.where(mine == (spots + start).astype(jnp.int16), one, zero)
                    for start in range(0, slab_rows, lane_width)
                ],
                axis=1,
            )
            term = jnp.dot(chosen, source, preferred_element_type=jnp.float32)
            if first:
                total[at, :] = term
            else:
                total[at, :] += term
            return carry

        lax.fori_loop(0, rows // tile, one_tile, 0)

    merge(1, slabs[1], True)
    for lane in (2, 0, 3):
        lane_copy(lane).wait()
        merge(lane, arrived[lane], False)
    merged[...] = total[...].astype(jnp.bfloat16)

    patches = (rows - PATCH) // PATCH
    half = parts // patches
    patch, place = part // half, lax.rem(part, half)
    last = patches - 1

    def rows_of(which):
        return pl.ds(pl.multiple_of((which + 1) * PATCH, PATCH), PATCH)

    head_copy = pltpu.make_async_remote_copy(
        src_ref=merged.at[pl.ds(0, PATCH)],
        dst_ref=head_in,
        send_sem=head_send.at[0],
        recv_sem=head_recv.at[0],
        device_id=(lax.rem(brick - 1 + bricks, bricks), part),
        device_id_type=MESH,
    )
    head_copy.start()

    def far_target(step):
        return lax.rem(patch + step, patches)

    def far_copy(step):
        return pltpu.make_async_remote_copy(
            src_ref=merged.at[rows_of(far_target(step))],
            dst_ref=window_in.at[part],
            send_sem=far_send.at[step],
            recv_sem=far_recv.at[step],
            device_id=(brick, far_target(step) * half + place),
            device_id_type=MESH,
        )

    def near_copy(step, far_step):
        source = lax.rem(patch - far_step + patches, patches) * half + place
        return pltpu.make_async_remote_copy(
            src_ref=window_in.at[source],
            dst_ref=window_in.at[source],
            send_sem=near_send.at[step, far_step],
            recv_sem=near_recv.at[step, far_step],
            device_id=(brick, patch * half + lax.rem(place + step, half)),
            device_id_type=MESH,
        )

    def start_far(late):
        for step in range(1, patches):

            @pl.when((far_target(step) == last) if late else (far_target(step) != last))
            def _():
                far_copy(step).start()

    def start_own():
        window_in[part] = merged[rows_of(patch), :]
        for step in range(1, half):
            near_copy(step, 0).start()

    start_far(False)

    @pl.when(patch != last)
    def _():
        start_own()

    head_copy.wait_recv()
    merged[rows - PATCH :, :] += head_in[...]
    start_far(True)

    @pl.when(patch == last)
    def _():
        start_own()

    for far_step in range(1, patches):
        far_copy(far_step).wait()
        for step in range(1, half):
            near_copy(step, far_step).start()
    for far_step in range(patches):
        for step in range(1, half):
            near_copy(step, far_step).wait()
    head_copy.wait_send()
    for source in range(parts):
        patch_rows[:, source * width : (source + 1) * width] = window_in[source]


def enter(index, slabs, bricks, parts):
    lanes, slab_rows, width = slabs.shape
    rows = index.shape[1]
    whole = pl.BlockSpec(memory_space=pltpu.VMEM)
    return pl.pallas_call(
        functools.partial(enter_kernel, bricks, parts),
        out_shape=jax.ShapeDtypeStruct((PATCH, width * parts), jnp.bfloat16),
        in_specs=[whole, whole],
        out_specs=whole,
        scratch_shapes=[
            pltpu.VMEM((lanes, slab_rows, width), jnp.bfloat16),
            pltpu.VMEM((rows, width), jnp.float32),
            pltpu.VMEM((rows, width), jnp.bfloat16),
            pltpu.VMEM((parts, PATCH, width), jnp.bfloat16),
            pltpu.VMEM((PATCH, width), jnp.bfloat16),
            pltpu.VMEM((rows, 128), jnp.int16),
            pltpu.SemaphoreType.DMA((lanes,)),
            pltpu.SemaphoreType.DMA((lanes,)),
            pltpu.SemaphoreType.DMA((parts,)),
            pltpu.SemaphoreType.DMA((parts,)),
            pltpu.SemaphoreType.DMA((parts, parts)),
            pltpu.SemaphoreType.DMA((parts, parts)),
            pltpu.SemaphoreType.DMA((1,)),
            pltpu.SemaphoreType.DMA((1,)),
        ],
        compiler_params=pltpu.CompilerParams(
            collective_id=0, has_side_effects=True, vmem_limit_bytes=VMEM_BYTES
        ),
        cost_estimate=pl.CostEstimate(
            flops=2 * rows * lanes * slab_rows * width,
            bytes_accessed=20 * slab_rows * width * lanes,
            transcendentals=0,
        ),
    )(index, slabs)


def leave_kernel(
    bricks,
    parts,
    index,
    result,
    arrived,
    rows_in,
    leaving,
    total,
    window_send,
    window_recv,
    tail_send,
    tail_recv,
    lane_send,
    lane_recv,
):
    brick, part = lax.axis_index("brick"), lax.axis_index("mp")
    lanes, slab_rows, width = leaving.shape
    quarter = result.shape[1]
    rows = rows_in.shape[0]
    last = rows - PATCH
    greet_all(bricks, parts)

    def row_start(source):
        return PATCH + source * quarter

    tail_copy = pltpu.make_async_remote_copy(
        src_ref=rows_in.at[pl.ds(last, PATCH)],
        dst_ref=rows_in.at[pl.ds(0, PATCH)],
        send_sem=tail_send.at[0],
        recv_sem=tail_recv.at[0],
        device_id=(lax.rem(brick + 1, bricks), part),
        device_id_type=MESH,
    )

    def window_copy(step):
        target = lax.rem(part + step, parts)
        start = pl.multiple_of(row_start(part), quarter)
        return pltpu.make_async_remote_copy(
            src_ref=result.at[target],
            dst_ref=rows_in.at[pl.ds(start, quarter)],
            send_sem=window_send.at[step],
            recv_sem=window_recv.at[step],
            device_id=(brick, target),
            device_id_type=MESH,
        )

    def window_arrival(step):
        source = lax.rem(part - step + parts, parts)
        return pltpu.make_async_remote_copy(
            src_ref=result.at[0],
            dst_ref=rows_in.at[pl.ds(pl.multiple_of(row_start(source), quarter), quarter)],
            send_sem=window_send.at[step],
            recv_sem=window_recv.at[step],
            device_id=(brick, source),
            device_id_type=MESH,
        )

    for step in range(1, parts):
        window_copy(step).start()
    rows_in[pl.ds(pl.multiple_of(row_start(part), quarter), quarter), :] = result[part]
    for step in range(1, parts):
        window_arrival(step).wait_recv()
    tail_copy.start()
    def lane_copy(lane):
        return pltpu.make_async_remote_copy(
            src_ref=leaving.at[lane],
            dst_ref=arrived.at[lane],
            send_sem=lane_send.at[lane],
            recv_sem=lane_recv.at[lane],
            device_id=(lax.rem(brick + lane - 1 + bricks, bricks), part),
            device_id_type=MESH,
        )

    def spread(lane, start, stop):
        spots = lax.broadcasted_iota(jnp.int32, (slab_rows, stop - start), 0)
        mine = (index[:, start:stop] - lane * slab_rows).astype(jnp.int16)
        one, zero = jnp.ones((), jnp.bfloat16), jnp.zeros((), jnp.bfloat16)
        chosen = jnp.where(mine == spots.astype(jnp.int16), one, zero)
        return jnp.dot(chosen, rows_in[start:stop, :], preferred_element_type=jnp.float32)

    for lane in (3, 0, 2):
        total[lane] = spread(lane, PATCH, rows)
    tail_copy.wait_recv()
    for lane in (3, 0, 2):
        leaving[lane] = (total[lane] + spread(lane, 0, PATCH)).astype(jnp.bfloat16)
        lane_copy(lane).start()
    arrived[1] = spread(1, 0, rows).astype(jnp.bfloat16)
    for lane in (2, 0, 3):
        lane_copy(lane).wait()

    for step in range(1, parts):
        window_copy(step).wait_send()

    tail_copy.wait_send()


def leave(index, result, bricks, lanes, slab_rows):
    parts, quarter, width = result.shape
    rows = index.shape[1]
    whole = pl.BlockSpec(memory_space=pltpu.VMEM)
    return pl.pallas_call(
        functools.partial(leave_kernel, bricks, parts),
        out_shape=jax.ShapeDtypeStruct((lanes, slab_rows, width), jnp.bfloat16),
        in_specs=[whole, whole],
        out_specs=whole,
        scratch_shapes=[
            pltpu.VMEM((rows, width), jnp.bfloat16),
            pltpu.VMEM((lanes, slab_rows, width), jnp.bfloat16),
            pltpu.VMEM((lanes, slab_rows, width), jnp.float32),
            pltpu.SemaphoreType.DMA((parts,)),
            pltpu.SemaphoreType.DMA((parts,)),
            pltpu.SemaphoreType.DMA((parts,)),
            pltpu.SemaphoreType.DMA((parts,)),
            pltpu.SemaphoreType.DMA((lanes,)),
            pltpu.SemaphoreType.DMA((lanes,)),
        ],
        compiler_params=pltpu.CompilerParams(
            collective_id=1, has_side_effects=True, vmem_limit_bytes=VMEM_BYTES
        ),
        cost_estimate=pl.CostEstimate(
            flops=2 * rows * lanes * slab_rows * width,
            bytes_accessed=20 * slab_rows * width * lanes,
            transcendentals=0,
        ),
    )(index, result)


def cut_kernel(starts, voxel_feats, slabs, held, arrived):
    part = lax.axis_index("mp")
    lanes, slab_rows, width = slabs.shape
    held_rows = held.shape[1]

    def copy(lane):
        first = pl.multiple_of(starts[1, lane], ALIGN)
        column = pl.multiple_of(part * width, width)
        return pltpu.make_async_copy(
            voxel_feats.at[pl.ds(first, held_rows), pl.ds(column, width)],
            held.at[lane],
            arrived.at[lane],
        )

    for lane in range(lanes):
        copy(lane).start()
    for lane in range(lanes):
        copy(lane).wait()
        rows = held[lane].astype(jnp.float32)
        ahead = starts[0, lane] - starts[1, lane]
        turned = pltpu.roll(rows, lax.rem(held_rows - ahead, held_rows), 0)
        slabs[lane] = turned[:slab_rows].astype(jnp.bfloat16)


def cut(starts, voxel_feats, slab_rows, parts):
    lanes = starts.shape[1]
    width = voxel_feats.shape[1] // parts
    return pl.pallas_call(
        cut_kernel,
        out_shape=jax.ShapeDtypeStruct((lanes, slab_rows, width), jnp.bfloat16),
        in_specs=[pl.BlockSpec(memory_space=pltpu.SMEM), pl.BlockSpec(memory_space=pl.ANY)],
        out_specs=pl.BlockSpec(memory_space=pltpu.VMEM),
        scratch_shapes=[
            pltpu.VMEM((lanes, slab_rows + ALIGN, width), jnp.bfloat16),
            pltpu.SemaphoreType.DMA((lanes,)),
        ],
        compiler_params=pltpu.CompilerParams(vmem_limit_bytes=VMEM_BYTES),
    )(starts, voxel_feats)


def place_kernel(starts, slabs, out, total):
    lanes, slab_rows, width = slabs.shape
    total[...] = jnp.zeros_like(total)
    for lane in range(lanes):
        rows = jnp.concatenate(
            [slabs[lane].astype(jnp.float32), jnp.zeros((ALIGN, width), jnp.float32)], axis=0
        )
        turned = pltpu.roll(rows, starts[0, lane] - starts[1, lane], 0)
        at = pl.ds(pl.multiple_of(starts[1, lane], ALIGN), slab_rows + ALIGN)
        total[at, :] += turned
    out[...] = total[...].astype(jnp.bfloat16)


def place(starts, slabs, capacity):
    width = slabs.shape[2]
    whole = pl.BlockSpec(memory_space=pltpu.VMEM)
    return pl.pallas_call(
        place_kernel,
        out_shape=jax.ShapeDtypeStruct((capacity, width), jnp.bfloat16),
        in_specs=[pl.BlockSpec(memory_space=pltpu.SMEM), whole],
        out_specs=whole,
        scratch_shapes=[pltpu.VMEM((capacity, width), jnp.float32)],
        compiler_params=pltpu.CompilerParams(vmem_limit_bytes=VMEM_BYTES),
    )(starts, slabs)


def layer_norm(values, gain):
    centred = values - jnp.mean(values, axis=-1, keepdims=True)
    spread = jnp.mean(centred * centred, axis=-1, keepdims=True)
    return (centred * lax.rsqrt(spread + EPSILON) * gain).astype(jnp.bfloat16)


def attention_kernel(
    head_dim,
    query_tile,
    query_from,
    patch_rows,
    gain,
    weights,
    attended,
    normed,
    queries,
    keys,
    values,
    held,
    mixed,
    arrived,
):
    groups, depth, triple = held.shape

    def copy(group):
        return pltpu.make_async_copy(
            weights.at[pl.ds(group * depth, depth)], held.at[group], arrived.at[group]
        )

    mixed[...] = jnp.zeros_like(mixed)
    for group in range(groups):
        copy(group).start()
    lanes = triple // 3
    group_heads = lanes // head_dim
    query_rows = attended.shape[0]
    normed[...] = layer_norm(patch_rows[...].astype(jnp.float32), gain[...])
    start = pl.multiple_of(query_from[0], query_rows)
    scale = head_dim ** (-0.5) * math.log2(math.e)
    lane_head = lax.broadcasted_iota(jnp.int32, (1, lanes), 1) // head_dim
    for group in range(groups):
        copy(group).wait()
        weight = held[group]
        queries[group] = (
            jnp.dot(
                normed[pl.ds(start, query_rows), :],
                weight[:, :lanes],
                preferred_element_type=jnp.float32,
            )
            * scale
        ).astype(jnp.bfloat16)
        both = jnp.dot(
            normed[...], weight[:, lanes:], preferred_element_type=jnp.float32
        ).astype(jnp.bfloat16)
        keys[group] = both[:, :lanes]
        values[group, :, :lanes] = both[:, lanes:]
        values[group, :, lanes:] = jnp.ones_like(both[:, lanes:])

    heads_once = group_heads
    chunks = query_rows // query_tile

    def some_heads(turn, carry):
        group = turn // (group_heads // heads_once)
        first_head = lax.rem(turn, group_heads // heads_once) * heads_once
        work = [(head, chunk) for head in range(heads_once) for chunk in range(chunks)]

        def rows_at(chunk):
            return slice(chunk * query_tile, (chunk + 1) * query_tile)

        def score(head, chunk):
            query = queries[group, rows_at(chunk), :]
            query = jnp.where(lane_head == first_head + head, query, jnp.zeros_like(query))
            return lax.dot_general(
                query,
                keys[group],
                (((1,), (1,)), ((), ())),
                preferred_element_type=jnp.float32,
            )

        def finish(head, chunk, exps):
            product = jnp.dot(exps, values[group], preferred_element_type=jnp.float32)
            result = product[:, :lanes] / product[:, lanes:]
            mine = lane_head == first_head + head
            at = rows_at(chunk)
            mixed[group, at, :] = jnp.where(mine, result, mixed[group, at, :])

        scores, exps = score(*work[0]), None
        for step, item in enumerate(work):
            later = score(*work[step + 1]) if step + 1 < len(work) else None
            highest = jnp.max(scores, axis=-1, keepdims=True)
            now = jnp.exp2((scores - highest).astype(jnp.bfloat16))
            if step:
                finish(*work[step - 1], exps)
            scores, exps = later, now
        finish(*work[-1], exps)
        return carry

    lax.fori_loop(0, groups * group_heads // heads_once, some_heads, 0)
    for group in range(groups):
        attended[:, group * lanes : (group + 1) * lanes] = mixed[group].astype(jnp.bfloat16)


def attention(patch_rows, gain, weights, query_from, query_rows, head_dim):
    rows, width = patch_rows.shape
    groups, triple = weights.shape[0] // width, weights.shape[1]
    lanes = triple // 3
    whole = pl.BlockSpec(memory_space=pltpu.VMEM)
    return pl.pallas_call(
        functools.partial(attention_kernel, head_dim, query_rows // 2),
        out_shape=jax.ShapeDtypeStruct((query_rows, groups * lanes), jnp.bfloat16),
        in_specs=[
            pl.BlockSpec(memory_space=pltpu.SMEM),
            whole,
            whole,
            pl.BlockSpec(memory_space=pl.ANY),
        ],
        out_specs=whole,
        scratch_shapes=[
            pltpu.VMEM((rows, width), jnp.bfloat16),
            pltpu.VMEM((groups, query_rows, lanes), jnp.bfloat16),
            pltpu.VMEM((groups, rows, lanes), jnp.bfloat16),
            pltpu.VMEM((groups, rows, 2 * lanes), jnp.bfloat16),
            pltpu.VMEM((groups, width, triple), jnp.bfloat16),
            pltpu.VMEM((groups, query_rows, lanes), jnp.float32),
            pltpu.SemaphoreType.DMA((groups,)),
        ],
        compiler_params=pltpu.CompilerParams(vmem_limit_bytes=VMEM_BYTES),
        cost_estimate=pl.CostEstimate(
            flops=4 * rows * query_rows * groups * lanes * 16,
            bytes_accessed=4 * rows * width,
            transcendentals=rows * query_rows * groups * 8,
        ),
    )(query_from, patch_rows, gain, weights)


def mlp_kernel(scalars, patch_rows, attended, gain, *refs):
    weights, result = refs[:-1], refs[-1]
    groups = len(weights)
    rows = attended.shape[0]
    depth = attended.shape[1] // groups
    hidden_part = (weights[0].shape[0] - depth) // 2
    proj_weight = [weights[group][:depth, :] for group in range(groups)]
    up_weight = [weights[group][depth : depth + hidden_part, :] for group in range(groups)]
    down_weight = [weights[group][depth + hidden_part :, :] for group in range(groups)]
    start = pl.multiple_of(scalars[0], rows)
    own = patch_rows[pl.ds(start, rows), :].astype(jnp.float32)
    mixed = None
    for group in range(groups):
        term = jnp.dot(
            attended[:, pl.ds(pl.multiple_of(scalars[1 + group] * depth, depth), depth)],
            proj_weight[group],
            preferred_element_type=jnp.float32,
        ).astype(jnp.bfloat16).astype(jnp.float32)
        mixed = term if mixed is None else mixed + term
    hidden = (own + mixed).astype(jnp.bfloat16).astype(jnp.float32)
    normed = layer_norm(hidden, gain[...])

    def widen(group):
        return jnp.dot(normed, up_weight[group], preferred_element_type=jnp.float32)

    total, expanded = None, widen(0)
    for group in range(groups):
        later = widen(group + 1) if group + 1 < groups else None
        expanded = (
            0.5 * expanded * (1.0 + lax.erf(expanded * math.sqrt(0.5)))
        ).astype(jnp.bfloat16)
        term = jnp.dot(
            expanded, down_weight[group], preferred_element_type=jnp.float32
        ).astype(jnp.bfloat16).astype(jnp.float32)
        total = term if total is None else total + term
        expanded = later
    final = (hidden + total).astype(jnp.bfloat16)
    width = result.shape[2]
    for part in range(result.shape[0]):
        result[part] = final[:, part * width : (part + 1) * width]


def mlp(patch_rows, attended, gain, weights, scalars):
    whole = pl.BlockSpec(memory_space=pltpu.VMEM)
    rows, width = attended.shape
    groups, hidden = len(weights), weights[0].shape[1]
    return pl.pallas_call(
        mlp_kernel,
        out_shape=jax.ShapeDtypeStruct((groups, rows, width // groups), jnp.bfloat16),
        in_specs=[pl.BlockSpec(memory_space=pltpu.SMEM)] + [whole] * (3 + groups),
        out_specs=whole,
        compiler_params=pltpu.CompilerParams(vmem_limit_bytes=VMEM_BYTES),
        cost_estimate=pl.CostEstimate(
            flops=4 * rows * width * hidden * groups,
            bytes_accessed=8 * width * hidden * groups,
            transcendentals=rows * hidden * groups,
        ),
    )(scalars, patch_rows, attended, gain, *weights)


def per_device(
    voxel_feats,
    slot_rank,
    curve_order,
    patch_shift,
    qkv_weight,
    proj_weight,
    up_weight,
    down_weight,
    norm_gains,
):
    bricks = lax.axis_size("brick")
    model_parts = lax.axis_size("mp")
    my_index = lax.axis_index("brick")
    part_index = lax.axis_index("mp")
    capacity = voxel_feats.shape[0]
    shard_rows = curve_order.shape[0]
    pair_rows = 3 * (shard_rows // 8)
    width_full = voxel_feats.shape[1]
    width_part = width_full // model_parts
    quarter_rows = shard_rows // model_parts
    head_dim = width_full // HEADS
    offset = patch_shift[0].astype(jnp.uint32)
    latest = capacity - pair_rows

    triple = qkv_weight.shape[1]
    spot = jnp.arange(triple, dtype=jnp.int32)
    kind, within = spot // width_part, spot % width_part
    origin = (within // head_dim) * 3 * head_dim + kind * head_dim + within % head_dim
    shuffle = (spot[:, None] == origin[None, :]).astype(jnp.bfloat16)
    qkv_sorted = jnp.dot(
        qkv_weight, shuffle, preferred_element_type=jnp.float32
    ).astype(jnp.bfloat16)
    qkv_all = lax.all_gather(qkv_sorted, "mp", axis=0, tiled=True)
    patches = shard_rows // PATCH
    half = model_parts // patches
    held = jnp.concatenate([proj_weight, up_weight, down_weight], axis=0)
    far = [held] + [passed(held, patches, step, 0) for step in range(1, patches)]

    lane_ids = jnp.arange(4, dtype=jnp.int32)
    lane_targets = wrapped(my_index - (lane_ids - 1), bricks)
    low = lane_targets * shard_rows
    below = slot_rank[:, None] < low[None, :]
    run_starts = jnp.sum(below.astype(jnp.int32), axis=0)
    slab_starts = jnp.minimum(run_starts, latest)
    aligned = jnp.minimum(slab_starts // ALIGN * ALIGN, latest - ALIGN)
    starts = jnp.stack([slab_starts, aligned])

    source_brick = curve_order // capacity
    source_slot = curve_order - source_brick * capacity
    source_lane = wrapped(source_brick - my_index + 1, bricks)
    from_lane = source_lane[:, None] == lane_ids[None, :]
    first_slot = jnp.min(jnp.where(from_lane, source_slot[:, None], latest), axis=0)
    first_of_row = jnp.sum(jnp.where(from_lane, first_slot[None, :], 0), axis=1)
    recv_index = source_lane * pair_rows + source_slot - first_of_row
    empty = jnp.full((PATCH,), -1, jnp.int32)
    index = lax.dynamic_slice_in_dim(
        jnp.concatenate([empty, recv_index, empty]), offset, shard_rows + PATCH, 0
    )

    slabs = cut(starts, voxel_feats, pair_rows, model_parts)
    patch_rows = enter(index[None, :], slabs, bricks, model_parts)
    *far, patch_rows = lax.optimization_barrier((*far, patch_rows))
    weights, origins = [], []
    for near_step in range(half):
        for patch_step in range(patches):
            value = far[patch_step]
            weights.append(passed(value, patches, 0, near_step) if near_step else value)
            patch = lax.rem(part_index // half + patches - patch_step, patches)
            place_in = lax.rem(part_index + half - near_step, half)
            origins.append(patch * half + place_in)
    query_from = (lax.rem(part_index * quarter_rows, PATCH))[None]
    attended = attention(
        patch_rows, norm_gains[0:1], qkv_all, query_from, quarter_rows, head_dim
    )
    scalars = jnp.concatenate([query_from, jnp.stack(origins)])
    result = mlp(patch_rows, attended, norm_gains[1:2], weights, scalars)
    returned = leave(index[None, :], result, bricks, 4, pair_rows)
    return place(starts, returned, capacity)


def solution(mesh):
    return jax.shard_map(
        per_device,
        mesh=mesh,
        in_specs=(
            P("brick", None),
            P("brick"),
            P("brick"),
            P(),
            P(None, "mp"),
            P("mp", None),
            P(None, "mp"),
            P("mp", None),
            P(),
        ),
        out_specs=P("brick", "mp"),
        check_vma=False,
    )
```
